256 devices in a mesh: slab: 64 (over z, y, core), tile: 4 (over x).
Axes of the slice: x: 4, y: 4, z: 8, core: 2. Of those that a mesh axis runs over, the one named last changes fastest.
Arguments:
- snapshots: bfloat16 [8192, 128, 256], P(('slab', 'tile')), may hold values from -1210 to 1210
- routes: int32 [8192, 1], P(('slab', 'tile')), may hold values from 0 to 3; in each aligned block of 32 rows (0 to 31, 32 to 63, ...) at most 10 rows name the same one
- sketch_matrix: bfloat16 [256, 128], replicated, may hold values from -0.375 to 0.375
Outputs:
- basis_rows: bfloat16 [10240, 128, 128], P(('slab', 'tile'))
- triangle: float32 [128, 128], replicated
The draws below stay inside these ranges and needn't reach their ends.
Inputs may be any that keep to these rules, and one draw needn't show every extreme that they name: `routes`: among the 32 blocks of one device no owner value appears more than 10 times; a block with value o goes to tile o of its own slab.
All inputs are finite; a program needn't handle non-finite values.
Results may differ from the reference program's by a relative error of at most 0.0065.
Values may be sent and summed in bfloat16 or wider, within the bound.
A program may use at most 64 MiB of HBM per device.

```python
import math
import jax
import jax.numpy as jnp
import numpy as np
from jax import lax

SNAP = 256
SKETCH = 128
BLK = 128
LOC = 32
SEND = 10
BLOCKS = 8192
SLOTS = 10240
CELLS = 1048576
N_SLAB = 64
N_TILE = 4


def draw_snapshots(key, part):
    key = jax.random.fold_in(key, 11)
    first_key = jax.random.fold_in(key, 0)
    second_key = jax.random.fold_in(key, 1)
    fourth_key = jax.random.fold_in(key, 3)
    fifth_key = jax.random.fold_in(key, 4)
    position = jnp.arange(BLOCKS, dtype=jnp.float32)
    trend_scale = jnp.exp(jnp.log(3.0) * position / BLOCKS)[:, None, None]
    slab_count = BLOCKS // (LOC * N_TILE)
    directions = jnp.clip(jax.random.normal(fourth_key, (slab_count, SNAP), dtype=jnp.float32), -3.0, 3.0) / math.sqrt(SNAP)
    slab_of_block = jnp.arange(BLOCKS, dtype=jnp.int32) // (LOC * N_TILE)
    block_direction = jnp.take(directions, slab_of_block, axis=0)[:, None, :]
    row_weight = jnp.clip(jax.random.normal(fifth_key, (BLOCKS, BLK, 1), dtype=jnp.float32), -3.0, 3.0)
    aligned = 12.0 * row_weight * block_direction
    spread = jnp.exp(jax.random.uniform(first_key, (BLOCKS, 1, 1), dtype=jnp.float32) * jnp.log(10.0))
    values = jnp.clip(jax.random.normal(second_key, (BLOCKS, BLK, SNAP), dtype=jnp.float32), -6.0, 6.0)
    return ((values + aligned) * spread * trend_scale).astype(jnp.bfloat16)


def routed_block(key, own, number, rows, number_of, top, reach, skew):
    ranking = jax.random.permutation(key, number_of)
    crowded, usual = load_shares(number_of, rows * top, reach, skew, True), load_shares(number_of, rows * top, reach, skew, False)
    places = jnp.arange(number_of)

    def named(lengths, turn):
        used = int((lengths > 0).sum())
        fixed = max(1, used // 4)
        shifted = fixed + (places - fixed + turn * (used - fixed)) % max(1, number_of - fixed)
        return jnp.zeros((number_of,), jnp.int32).at[ranking[jnp.where(places < fixed, places, shifted)]].set(jnp.asarray(lengths, jnp.int32))

    lengths = jnp.where(number % 4 == 0, named(crowded, number // 4), named(usual, number - number // 4 - 1))
    mixed = jax.random.permutation(jax.random.fold_in(own, 3), number_of)
    donor, taker = mixed[0:number_of // 2 * 2:2], mixed[1:number_of // 2 * 2:2]
    slack = jnp.minimum(lengths[donor] - 1, reach - lengths[taker]) // 2
    slack = jnp.where((donor == ranking[0]) | (taker == ranking[0]) | (lengths[taker] == 0), 0, jnp.maximum(slack, 0))
    shifted = jax.random.randint(jax.random.fold_in(own, 4), (number_of // 2,), 0, 1 << 20) % (slack + 1)
    lengths = lengths.at[donor].add(-shifted).at[taker].add(shifted)
    labels = jnp.searchsorted(jnp.cumsum(lengths), jnp.arange(rows * top), side="right").astype(jnp.int32)
    table = labels.reshape(top, rows).T
    table = table[jax.random.permutation(jax.random.fold_in(own, 1), rows)]
    turn = jax.random.randint(jax.random.fold_in(own, 2), (rows, 1), 0, top)
    return jnp.take_along_axis(table, (jnp.arange(top)[None, :] + turn) % top, axis=1)


def load_shares(number_of, total, limit, lean, full):
    loads = [(1 << 20) // math.isqrt(grade ** lean) + 1 for grade in range(1, number_of + 1)]
    largest = limit if full else min(limit, max(-(-total // number_of), total * loads[0] // sum(loads)))
    least = 1 if total - largest >= number_of - 1 else 0
    given, rest = [largest] + [least] * (number_of - 1), total - largest - least * (number_of - 1)
    while rest > 0:
        candidates = [i for i in range(1, number_of) if given[i] < largest] or [i for i in range(1, number_of) if given[i] < limit]
        whole, budget = sum([loads[i] for i in candidates]), rest
        for i in candidates:
            extra = min(limit - given[i], max(1, budget * loads[i] // whole), rest)
            given[i] = given[i] + extra
            rest = rest - extra
    return np.array(given)


def gaussian(rng, dims, scale, bound, held_as=jnp.bfloat16):
    drawn = jax.random.normal(rng, dims, jnp.float32) * scale
    return jnp.minimum(jnp.maximum(drawn, -bound), bound).astype(held_as)


def setup_inputs(seed: int = 0) -> dict:
    splits = jax.random.split(jax.random.key(seed), 4)
    snapshots = draw_snapshots(jax.random.fold_in(splits[3], 71), 0)
    routes_keys = jax.random.split(jax.random.fold_in(splits[1], 1), BLOCKS // LOC)
    routes_turns = jax.random.permutation(jax.random.fold_in(splits[1], 3), BLOCKS // LOC)
    routes = jax.vmap(lambda own, number: routed_block(jax.random.fold_in(splits[1], 2), own, number, LOC, N_TILE, 1, SEND, 2))(routes_keys, routes_turns).reshape((BLOCKS, 1))
    sketch_matrix = gaussian(splits[2], (SNAP, SKETCH), SNAP ** -0.5, 0.375)
    return dict(snapshots=snapshots, routes=routes, sketch_matrix=sketch_matrix)


def owner_sketch(owner_index, snapshots, routes, sketch_matrix):
    slab_index = owner_index // N_TILE
    tile_index = owner_index % N_TILE
    first_block = (slab_index * (N_TILE * LOC)).astype(jnp.int32)
    source_blocks = lax.dynamic_slice_in_dim(snapshots, first_block, N_TILE * LOC, 0).reshape(N_TILE, LOC, BLK, SNAP)
    source_routes = lax.dynamic_slice_in_dim(routes[:, 0], first_block, N_TILE * LOC, 0).reshape(N_TILE, LOC)
    owner_hit = (source_routes == tile_index).astype(jnp.int32)
    earlier = jnp.cumsum(owner_hit, axis=1) - owner_hit
    slot_ids = jnp.arange(SEND, dtype=jnp.int32)
    chosen = owner_hit[:, None, :] * (earlier[:, None, :] == slot_ids[None, :, None]).astype(jnp.int32)
    positions = jnp.arange(LOC, dtype=jnp.int32)
    source_index = lax.optimization_barrier(jnp.sum(chosen * positions[None, None, :], axis=2)).astype(jnp.int32)
    present = lax.optimization_barrier(jnp.sum(chosen, axis=2))
    picked = jnp.take_along_axis(source_blocks, source_index[:, :, None, None], axis=1)
    placed = jnp.where(present[:, :, None, None] > 0, picked, jnp.zeros_like(picked))
    product = jnp.dot(placed.reshape(N_TILE * SEND * BLK, SNAP).astype(jnp.float32), sketch_matrix.astype(jnp.float32), preferred_element_type=jnp.float32)
    return product.astype(jnp.bfloat16)

def reference(snapshots, routes, sketch_matrix):
    owners = jnp.arange(N_SLAB * N_TILE, dtype=jnp.int32)

    def one_owner(owner_index):
        return owner_sketch(owner_index, snapshots, routes, sketch_matrix)
    sketches = lax.map(one_owner, owners)

    def accumulate(running, row_block):
        product = lax.dot_general(row_block.astype(jnp.float32), row_block.astype(jnp.float32), (((0,), (0,)), ((), ())), preferred_element_type=jnp.float32)
        return (running + product, None)
    gram_matrix, unused = lax.scan(accumulate, jnp.zeros((SKETCH, SKETCH), jnp.float32), sketches)
    lower_factor = jnp.linalg.cholesky(gram_matrix)
    identity = jnp.eye(SKETCH, dtype=jnp.float32)
    inverse_factor = jax.scipy.linalg.solve_triangular(lower_factor, identity, lower=True)
    cell_root = math.sqrt(CELLS)

    def one_basis(row_block):
        scaled = jnp.dot(row_block.astype(jnp.float32), inverse_factor.T, precision=lax.Precision.HIGHEST) * cell_root
        return scaled.astype(jnp.bfloat16)
    basis_rows = lax.map(one_basis, sketches)
    return (basis_rows.reshape(SLOTS, BLK, SKETCH), lower_factor.T / cell_root)
```

```python
import functools
import math

import jax
import jax.numpy as jnp
from jax import lax
from jax.experimental import pallas as pl
from jax.experimental.pallas import tpu as pltpu
from jax.sharding import PartitionSpec as P

SEND = 10
TILES = 4
GROUP = 16
PIECES = 8
MESH = pl.DeviceIdType.MESH


def exchange(routes_ref, x_hbm, s_ref, placed_ref, gram_ref, x_ref, sk_ref, send_ref, part_ref, got1_ref, got2_ref,
             table_ref, x_sem, put_sem, get_sem, ar_put, ar_get):
    slab, tile = lax.axis_index("slab"), lax.axis_index("tile")
    core, y, z = slab % 2, (slab // 2) % 4, slab // 8
    ring = z * 2 + core
    face = y * 4 + tile

    def ring_peer(k):
        return (((k // 2) * 4 + y) * 2 + k % 2, tile)

    def face_peer(k):
        return ((z * 4 + k // 4) * 2 + core, k % 4)

    rows = x_hbm.shape[0] // PIECES

    def piece(p):
        part = pl.ds(p * rows, rows)
        return pltpu.make_async_copy(x_hbm.at[part], x_ref.at[part], x_sem.at[p])

    for p in range(PIECES):
        piece(p).start()

    barrier = pltpu.get_barrier_semaphore()

    @pl.loop(1, GROUP)
    def _(d):
        pl.semaphore_signal(barrier, inc=1, device_id=ring_peer((ring + d) % GROUP), device_id_type=MESH)
        pl.semaphore_signal(barrier, inc=1, device_id=face_peer((face + d) % GROUP), device_id_type=MESH)

    masks = [jnp.int32(0)] * TILES
    for j in range(32):
        route = routes_ref[0, j]
        bit = (1 << j) if j < 31 else -(1 << 31)
        masks = [jnp.where(route == o, m | jnp.int32(bit), m) for o, m in enumerate(masks)]
    for o in range(TILES):
        m = masks[o]
        for k in range(SEND):
            low = m & (-m)
            table_ref[o, k] = jnp.where(m != 0, 31 - lax.clz(low), -1)
            m = m & (m - 1)

    @pl.loop(0, PIECES)
    def _(p):
        piece(p).wait()
        wide = x_ref[pl.ds(p * rows, rows)].reshape(rows * 128, 256)
        sk = jnp.dot(wide, s_ref[...], preferred_element_type=jnp.float32)
        sk_ref[pl.ds(p * rows, rows)] = sk.astype(jnp.bfloat16).reshape(rows, 128, 128)

    pl.semaphore_wait(barrier, 2 * (GROUP - 1))

    def pick(o, k):
        at = table_ref[o, k]
        block = sk_ref[jnp.maximum(at, 0)]
        return jnp.where(at >= 0, block, jnp.zeros_like(block))

    def transfer(d):
        return pltpu.make_async_remote_copy(
            src_ref=send_ref.at[d - 1],
            dst_ref=placed_ref.at[tile],
            send_sem=put_sem.at[d - 1],
            recv_sem=get_sem.at[d - 1],
            device_id=(slab, (tile + d) % TILES),
            device_id_type=MESH,
        )

    for d in (2, 1, 3):
        @pl.loop(0, SEND)
        def _(k):
            send_ref[d - 1, k] = pick((tile + d) % TILES, k)
        transfer(d).start()

    part_ref[...] = jnp.zeros_like(part_ref)

    @pl.loop(0, PIECES)
    def _(p):
        sk = sk_ref[pl.ds(p * rows, rows)].reshape(rows * 128, 128)
        g = lax.dot_general(sk, sk, (((0,), (0,)), ((), ())), preferred_element_type=jnp.float32)
        part_ref[...] += g.reshape(GROUP, 8, 128)

    def all_of(ref, sem):
        return pltpu.make_async_copy(ref.at[pl.ds(0, GROUP - 1)], ref.at[pl.ds(0, GROUP - 1)], sem)

    def scatter(d):
        to = (ring + d) % GROUP
        return pltpu.make_async_remote_copy(
            src_ref=part_ref.at[to], dst_ref=got1_ref.at[d - 1], send_sem=ar_put.at[0], recv_sem=ar_get.at[0],
            device_id=ring_peer(to), device_id_type=MESH)

    @pl.loop(1, GROUP)
    def _(d):
        scatter(d).start()
    all_of(got1_ref, ar_get.at[0]).wait()
    mine = part_ref[ring]
    for d in range(GROUP - 1):
        mine = mine + got1_ref[d]
    got2_ref[face] = mine

    def swap(d):
        to = (face + d) % GROUP
        return pltpu.make_async_remote_copy(
            src_ref=got2_ref.at[face], dst_ref=got2_ref.at[face], send_sem=ar_put.at[1], recv_sem=ar_get.at[1],
            device_id=face_peer(to), device_id_type=MESH)

    @pl.loop(1, GROUP)
    def _(d):
        swap(d).start()
    all_of(got2_ref, ar_get.at[1]).wait()
    total = got2_ref[0]
    for d in range(1, GROUP):
        total = total + got2_ref[d]
    gram_ref[ring] = total

    def spread(d):
        to = (ring + d) % GROUP
        return pltpu.make_async_remote_copy(
            src_ref=gram_ref.at[ring], dst_ref=gram_ref.at[ring], send_sem=ar_put.at[2], recv_sem=ar_get.at[2],
            device_id=ring_peer(to), device_id_type=MESH)

    @pl.loop(1, GROUP)
    def _(d):
        spread(d).start()
    all_of(gram_ref, ar_get.at[2]).wait()

    @pl.loop(0, SEND)
    def _(k):
        placed_ref[tile, k] = pick(tile, k)
    for d in (1, 3, 2):
        transfer(d).wait()
    for i in range(3):
        all_of(got1_ref, ar_put.at[i]).wait()


def local(snapshots, routes, sketch_matrix):
    cell_root = math.sqrt(snapshots.shape[0] * 128 * lax.axis_size("slab") * lax.axis_size("tile"))
    vmem = pl.BlockSpec(memory_space=pltpu.VMEM)
    placed, gram = pl.pallas_call(
        exchange,
        out_shape=(
            jax.ShapeDtypeStruct((TILES, SEND, 128, 128), jnp.bfloat16),
            jax.ShapeDtypeStruct((GROUP, 8, 128), jnp.float32),
        ),
        in_specs=[pl.BlockSpec(memory_space=pltpu.SMEM), pl.BlockSpec(memory_space=pl.ANY), vmem],
        out_specs=(vmem, vmem),
        scratch_shapes=[
            pltpu.VMEM((32, 128, 256), jnp.bfloat16),
            pltpu.VMEM((32, 128, 128), jnp.bfloat16),
            pltpu.VMEM((TILES - 1, SEND, 128, 128), jnp.bfloat16),
            pltpu.VMEM((GROUP, 8, 128), jnp.float32),
            pltpu.VMEM((GROUP, 8, 128), jnp.float32),
            pltpu.VMEM((GROUP, 8, 128), jnp.float32),
            pltpu.SMEM((TILES, SEND), jnp.int32),
            pltpu.SemaphoreType.DMA((PIECES,)),
            pltpu.SemaphoreType.DMA((TILES - 1,)),
            pltpu.SemaphoreType.DMA((TILES - 1,)),
            pltpu.SemaphoreType.DMA((3,)),
            pltpu.SemaphoreType.DMA((3,)),
        ],
        compiler_params=pltpu.CompilerParams(collective_id=0, has_side_effects=True, vmem_limit_bytes=32 * 2**20),
        name="exchange",
    )(routes.reshape(1, 32), snapshots, sketch_matrix)
    lower = jnp.linalg.cholesky(gram.reshape(128, 128))
    inverse = jax.scipy.linalg.solve_triangular(lower, jnp.eye(128, dtype=jnp.float32), lower=True)
    rows = placed.reshape(-1, 128)
    basis = (jnp.dot(rows.astype(jnp.float32), inverse.T, precision=lax.Precision.HIGHEST) * cell_root).astype(jnp.bfloat16)
    return basis.reshape(TILES * SEND, 128, 128), lower.T / cell_root


def solution(mesh):
    return jax.shard_map(
        local,
        mesh=mesh,
        in_specs=(P(("slab", "tile"), None, None), P(("slab", "tile"), None), P()),
        out_specs=(P(("slab", "tile"), None, None), P()),
        check_vma=False,
    )
```

```python
import math

import jax
import jax.numpy as jnp
from jax import lax
from jax.experimental import pallas as pl
from jax.experimental.pallas import tpu as pltpu
from jax.sharding import PartitionSpec as P

SEND = 10
TILES = 4
GROUP = 16
PIECES = 8
STEPS = 8
FIRST = ((1, 0), (3, 0))
LATER = ((2, 0), (2, 1), (1, 1), (3, 1))
MESH = pl.DeviceIdType.MESH
F32, BF16 = jnp.float32, jnp.bfloat16


def split3(v):
    h = v.astype(BF16)
    rest = v - h.astype(F32)
    m = rest.astype(BF16)
    return h, m, (rest - m.astype(F32)).astype(BF16)


def outer_products(u):
    h, m, l = split3(u)
    left = jnp.concatenate([v[:, :128] for v in (h, h, m, h, l, m)], 0)
    right = jnp.concatenate([h, m, h, l, h, m], 0)
    return lax.dot_general(left, right, (((0,), (0,)), ((), ())), preferred_element_type=F32)


def factor(gram_ref, upper_ref, inverse_ref, work):
    row = lax.broadcasted_iota(jnp.int32, (128, 128), 0)
    col = lax.broadcasted_iota(jnp.int32, (128, 128), 1)
    work[:, :128] = gram_ref[...].reshape(128, 128)
    work[:, 128:] = (row == col).astype(F32)
    sub = lax.broadcasted_iota(jnp.int32, (8, 256), 0)
    for p in range(GROUP):
        panel = work[8 * p : 8 * p + 8, :]
        e = {}
        for k in range(8):
            c = jnp.broadcast_to(panel[:, 8 * p + k : 8 * p + k + 1], (8, 128))
            for i in range(k, 8):
                e[i, k] = jnp.broadcast_to(c[i : i + 1], (8, 128))
        x = [jnp.broadcast_to(panel[i : i + 1], (8, 256)) for i in range(8)]
        for k in range(8):
            r = lax.rsqrt(e[k, k])
            l = {i: e[i, k] * r for i in range(k + 1, 8)}
            x[k] = x[k] * jnp.concatenate([r, r], 1)
            for i in range(k + 1, 8):
                for j in range(k + 1, i + 1):
                    e[i, j] = e[i, j] - l[i] * l[j]
                x[i] = x[i] - jnp.concatenate([l[i], l[i]], 1) * x[k]
        u = x[0]
        for k in range(1, 8):
            u = jnp.where(sub == k, x[k], u)
        upper_ref[8 * p : 8 * p + 8, :] = u[:, :128]
        inverse_ref[8 * p : 8 * p + 8, :] = u[:, 128:]
        if p < GROUP - 1:
            g = outer_products(u)
            work[8 * p + 8 :, :] = work[8 * p + 8 :, :] - g[8 * p + 8 :, :]


def exchange(routes_hbm, x_hbm, s_hbm, placed_ref, upper_ref, inverse_ref, x_ref, s_ref, routes_ref, sk_ref, send_ref, part_ref,
             got1_ref, got2_ref, gram_ref, work_ref, table_ref, x_sem, in_sem, put_sem, get_sem, ar_put, ar_get):
    slab, tile = lax.axis_index("slab"), lax.axis_index("tile")
    core, y, z = slab % 2, (slab // 2) % 4, slab // 8
    ring = z * 2 + core
    face = y * 4 + tile

    def ring_peer(k):
        return (((k // 2) * 4 + y) * 2 + k % 2, tile)

    def face_peer(k):
        return ((z * 4 + k // 4) * 2 + core, k % 4)

    rows = x_hbm.shape[0] // PIECES

    def piece(p):
        part = pl.ds(p * rows, rows)
        return pltpu.make_async_copy(x_hbm.at[part], x_ref.at[part], x_sem.at[p])

    s_copy = pltpu.make_async_copy(s_hbm, s_ref, in_sem.at[0])
    routes_copy = pltpu.make_async_copy(routes_hbm, routes_ref, in_sem.at[1])
    s_copy.start()
    for p in range(PIECES):
        piece(p).start()
    routes_copy.start()

    barrier = pltpu.get_barrier_semaphore()
    for d in range(1, GROUP):
        pl.semaphore_signal(barrier, inc=1, device_id=ring_peer((ring + d) % GROUP), device_id_type=MESH)
        pl.semaphore_signal(barrier, inc=1, device_id=face_peer((face + d) % GROUP), device_id_type=MESH)

    part_ref[...] = jnp.zeros_like(part_ref)
    s_copy.wait()

    @pl.loop(0, PIECES)
    def _(p):
        piece(p).wait()
        wide = x_ref[pl.ds(p * rows, rows)].reshape(rows * 128, 256)
        sk = jnp.dot(wide, s_ref[...], preferred_element_type=F32).astype(BF16)
        sk_ref[pl.ds(p * rows, rows)] = sk.reshape(rows, 128, 128)
        g = lax.dot_general(sk, sk, (((0,), (0,)), ((), ())), preferred_element_type=F32)
        part_ref[...] += g.reshape(GROUP, 8, 128)

    pl.semaphore_wait(barrier, 2 * (GROUP - 1))

    def all_of(ref, sem):
        return pltpu.make_async_copy(ref.at[pl.ds(0, GROUP - 1)], ref.at[pl.ds(0, GROUP - 1)], sem)

    for d in range(1, GROUP):
        to = (ring + d) % GROUP
        pltpu.make_async_remote_copy(
            src_ref=part_ref.at[to], dst_ref=got1_ref.at[d - 1], send_sem=ar_put.at[0], recv_sem=ar_get.at[0],
            device_id=ring_peer(to), device_id_type=MESH).start()

    routes_copy.wait()
    masks = [jnp.int32(0)] * TILES
    for j in range(32):
        route = routes_ref[0, j]
        bit = (1 << j) if j < 31 else -(1 << 31)
        masks = [jnp.where(route == o, m | jnp.int32(bit), m) for o, m in enumerate(masks)]
    for o in range(TILES):
        m = masks[o]
        for k in range(SEND):
            low = m & (-m)
            table_ref[o, k] = jnp.where(m != 0, 31 - lax.clz(low), -1)
            m = m & (m - 1)

    def pick(o, k):
        at = table_ref[o, k]
        block = sk_ref[jnp.maximum(at, 0)]
        return jnp.where(at >= 0, block, jnp.zeros_like(block))

    half = SEND // 2

    def transfer(d, h):
        return pltpu.make_async_remote_copy(
            src_ref=send_ref.at[d - 1, pl.ds(h * half, half)],
            dst_ref=placed_ref.at[tile, pl.ds(h * half, half)],
            send_sem=put_sem.at[d - 1, h],
            recv_sem=get_sem.at[d - 1, h],
            device_id=(slab, (tile + d) % TILES),
            device_id_type=MESH,
        )

    def fill(d, h):
        @pl.loop(h * half, (h + 1) * half)
        def _(k):
            send_ref[d - 1, k] = pick((tile + d) % TILES, k)

    for d, h in FIRST:
        fill(d, h)
        transfer(d, h).start()
    for d, h in LATER:
        fill(d, h)

    @pl.loop(0, SEND)
    def _(k):
        placed_ref[tile, k] = pick(tile, k)

    all_of(got1_ref, ar_get.at[0]).wait()
    mine = part_ref[ring]
    for d in range(GROUP - 1):
        mine = mine + got1_ref[d]
    got2_ref[face] = mine
    for d in range(1, GROUP):
        to = (face + d) % GROUP
        pltpu.make_async_remote_copy(
            src_ref=got2_ref.at[face], dst_ref=got2_ref.at[face], send_sem=ar_put.at[1], recv_sem=ar_get.at[1],
            device_id=face_peer(to), device_id_type=MESH).start()
    all_of(got2_ref, ar_get.at[1]).wait()
    total = got2_ref[0]
    for d in range(1, GROUP):
        total = total + got2_ref[d]
    gram_ref[ring] = total
    for d in range(1, GROUP):
        to = (ring + d) % GROUP
        pltpu.make_async_remote_copy(
            src_ref=gram_ref.at[ring], dst_ref=gram_ref.at[ring], send_sem=ar_put.at[2], recv_sem=ar_get.at[2],
            device_id=ring_peer(to), device_id_type=MESH).start()
    for d, h in LATER:
        transfer(d, h).start()
    all_of(gram_ref, ar_get.at[2]).wait()

    factor(gram_ref, upper_ref, inverse_ref, work_ref)

    for i in range(3):
        all_of(got1_ref, ar_put.at[i]).wait()
    for d, h in FIRST + LATER:
        transfer(d, h).wait()


def scale(cell_root, placed_ref, upper_ref, inverse_ref, basis_hbm, triangle_hbm, basis_ref, triangle_ref, sem, tri_sem):
    row = lax.broadcasted_iota(jnp.int32, (128, 128), 0)
    col = lax.broadcasted_iota(jnp.int32, (128, 128), 1)
    triangle_ref[...] = jnp.where(row <= col, upper_ref[...] * (1.0 / cell_root), 0.0)
    tri = pltpu.make_async_copy(triangle_ref, triangle_hbm, tri_sem)
    tri.start()
    h, m, l = split3(jnp.where(row >= col, inverse_ref[...] * cell_root, 0.0))
    count = placed_ref.shape[0] // STEPS

    def copy(i):
        part = pl.ds(i * count, count)
        return pltpu.make_async_copy(basis_ref.at[part], basis_hbm.at[part], sem.at[i])

    for i in range(STEPS):
        part = pl.ds(i * count, count)
        rows = placed_ref[part].reshape(count * 128, 128)
        out = sum(lax.dot_general(rows, w, (((1,), (1,)), ((), ())), preferred_element_type=F32) for w in (l, m, h))
        basis_ref[part] = out.astype(BF16).reshape(count, 128, 128)
        copy(i).start()
    tri.wait()
    for i in range(STEPS):
        copy(i).wait()


def local(snapshots, routes, sketch_matrix):
    cell_root = math.sqrt(snapshots.shape[0] * 128 * lax.axis_size("slab") * lax.axis_size("tile"))
    vmem = pl.BlockSpec(memory_space=pltpu.VMEM)
    hbm = pl.BlockSpec(memory_space=pltpu.HBM)
    square = jax.ShapeDtypeStruct((128, 128), F32)
    placed, upper, inverse = pl.pallas_call(
        exchange,
        out_shape=(jax.ShapeDtypeStruct((TILES, SEND, 128, 128), BF16), square, square),
        in_specs=[hbm, hbm, hbm],
        out_specs=(vmem, vmem, vmem),
        scratch_shapes=[
            pltpu.VMEM((32, 128, 256), BF16),
            pltpu.VMEM((256, 128), BF16),
            pltpu.SMEM((1, 32), jnp.int32),
            pltpu.VMEM((32, 128, 128), BF16),
            pltpu.VMEM((TILES - 1, SEND, 128, 128), BF16),
            pltpu.VMEM((GROUP, 8, 128), F32),
            pltpu.VMEM((GROUP, 8, 128), F32),
            pltpu.VMEM((GROUP, 8, 128), F32),
            pltpu.VMEM((GROUP, 8, 128), F32),
            pltpu.VMEM((128, 256), F32),
            pltpu.SMEM((TILES, SEND), jnp.int32),
            pltpu.SemaphoreType.DMA((PIECES,)),
            pltpu.SemaphoreType.DMA((2,)),
            pltpu.SemaphoreType.DMA((TILES - 1, 2)),
            pltpu.SemaphoreType.DMA((TILES - 1, 2)),
            pltpu.SemaphoreType.DMA((3,)),
            pltpu.SemaphoreType.DMA((3,)),
        ],
        compiler_params=pltpu.CompilerParams(collective_id=0, has_side_effects=True, vmem_limit_bytes=32 * 2**20),
        name="exchange",
    )(*(pltpu.with_memory_space_constraint(v, pltpu.HBM) for v in (routes.reshape(1, 32), snapshots, sketch_matrix)))
    return tuple(pl.pallas_call(
        lambda *refs: scale(cell_root, *refs),
        out_shape=(jax.ShapeDtypeStruct((TILES * SEND, 128, 128), BF16), square),
        in_specs=[vmem, vmem, vmem],
        out_specs=(hbm, hbm),
        scratch_shapes=[
            pltpu.VMEM((TILES * SEND, 128, 128), BF16),
            pltpu.VMEM((128, 128), F32),
            pltpu.SemaphoreType.DMA((STEPS,)),
            pltpu.SemaphoreType.DMA,
        ],
        compiler_params=pltpu.CompilerParams(vmem_limit_bytes=32 * 2**20),
        name="scale",
    )(placed.reshape(TILES * SEND, 128, 128), upper, inverse))


def solution(mesh):
    return jax.shard_map(
        local,
        mesh=mesh,
        in_specs=(P(("slab", "tile"), None, None), P(("slab", "tile"), None), P()),
        out_specs=(P(("slab", "tile"), None, None), P()),
        check_vma=False,
    )
```

```python
import math

import jax
import jax.numpy as jnp
from jax import lax
from jax.experimental import pallas as pl
from jax.experimental.pallas import tpu as pltpu
from jax.sharding import PartitionSpec as P

SEND = 10
TILES = 4
GROUP = 16
PIECES = 8
STEPS = 8
SPAN = 64
START = (((2, 0, 5),), ((2, 5, 5), (1, 0, 10), (3, 0, 10)), ())
MESH = pl.DeviceIdType.MESH
F32, BF16 = jnp.float32, jnp.bfloat16


def split3(v):
    h = v.astype(BF16)
    rest = v - h.astype(F32)
    m = rest.astype(BF16)
    return h, m, (rest - m.astype(F32)).astype(BF16)


def outer_products(u):
    h, m, l = split3(u)
    left = jnp.concatenate([v[:, :128] for v in (h, h, m, h, l, m)], 0)
    right = jnp.concatenate([h, m, h, l, h, m], 0)
    return lax.dot_general(left, right, (((0,), (0,)), ((), ())), preferred_element_type=F32)


def line(v, i):
    return jnp.broadcast_to(v[i : i + 1], (8, v.shape[1]))


def columns(rows, p):
    return [jnp.broadcast_to(rows[:, p + k : p + k + 1], (8, 128)) for k in range(8)]


def wide(v):
    return jnp.concatenate([v, v], 1)


def factor(gram_ref, upper_ref, inverse_ref, work):
    row = lax.broadcasted_iota(jnp.int32, (128, 128), 0)
    col = lax.broadcasted_iota(jnp.int32, (128, 128), 1)
    work[:, :128] = gram_ref[...].reshape(128, 128)
    work[:, 128:] = (row == col).astype(F32)
    sub = lax.broadcasted_iota(jnp.int32, (8, 256), 0)
    for s in range(0, 128, SPAN):
        rows = {q: work[q : q + 8, :] for q in range(s, s + SPAN, 8)}
        own = columns(rows[s], s)
        done = []
        for p in range(s, s + SPAN, 8):
            later = range(p + 8, s + SPAN, 8)
            cols = {q: columns(rows[q], p) for q in later}
            e = {(i, k): line(own[k], i) for k in range(8) for i in range(k, 8)}
            own = columns(rows[p + 8], p + 8) if later else None
            x = [line(rows[p], i) for i in range(8)]
            for k in range(8):
                r = lax.rsqrt(e[k, k])
                l = {i: e[i, k] * r for i in range(k + 1, 8)}
                for i in range(k + 1, 8):
                    for j in range(k + 1, i + 1):
                        e[i, j] = e[i, j] - l[i] * l[j]
                x[k] = x[k] * wide(r)
                for i in range(k + 1, 8):
                    x[i] = x[i] - wide(l[i]) * x[k]
                for q in later:
                    m = cols[q][k] * r
                    if q == p + 8:
                        own = [o - m * line(m, j) for j, o in enumerate(own)]
                    for j in range(k + 1, 8):
                        cols[q][j] = cols[q][j] - m * l[j]
                    rows[q] = rows[q] - wide(m) * x[k]
            u = x[0]
            for k in range(1, 8):
                u = jnp.where(sub == k, x[k], u)
            upper_ref[p : p + 8, :] = u[:, :128]
            inverse_ref[p : p + 8, :] = u[:, 128:]
            done.append(u)
        if s + SPAN < 128:
            g = outer_products(jnp.concatenate(done, 0))
            work[s + SPAN :, :] = work[s + SPAN :, :] - g[s + SPAN :, :]


def exchange(routes_hbm, x_hbm, s_hbm, placed_ref, upper_ref, inverse_ref, x_ref, s_ref, routes_ref, sk_ref, send_ref, part_ref,
             got1_ref, got2_ref, gram_ref, work_ref, table_ref, x_sem, in_sem, put_sem, get_sem, ar_put, ar_get):
    slab, tile = lax.axis_index("slab"), lax.axis_index("tile")
    core, y, z = slab % 2, (slab // 2) % 4, slab // 8
    ring = z * 2 + core
    face = y * 4 + tile

    def ring_peer(k):
        return (((k // 2) * 4 + y) * 2 + k % 2, tile)

    def face_peer(k):
        return ((z * 4 + k // 4) * 2 + core, k % 4)

    rows = x_hbm.shape[0] // PIECES

    def piece(p):
        part = pl.ds(p * rows, rows)
        return pltpu.make_async_copy(x_hbm.at[part], x_ref.at[part], x_sem.at[p])

    s_copy = pltpu.make_async_copy(s_hbm, s_ref, in_sem.at[0])
    routes_copy = pltpu.make_async_copy(routes_hbm, routes_ref, in_sem.at[1])
    s_copy.start()
    for p in range(PIECES):
        piece(p).start()
    routes_copy.start()

    barrier = pltpu.get_barrier_semaphore()
    for d in range(1, GROUP):
        pl.semaphore_signal(barrier, inc=1, device_id=ring_peer((ring + d) % GROUP), device_id_type=MESH)
        pl.semaphore_signal(barrier, inc=1, device_id=face_peer((face + d) % GROUP), device_id_type=MESH)

    part_ref[...] = jnp.zeros_like(part_ref)
    s_copy.wait()

    @pl.loop(0, PIECES)
    def _(p):
        piece(p).wait()
        wide = x_ref[pl.ds(p * rows, rows)].reshape(rows * 128, 256)
        sk = jnp.dot(wide, s_ref[...], preferred_element_type=F32).astype(BF16)
        sk_ref[pl.ds(p * rows, rows)] = sk.reshape(rows, 128, 128)
        g = lax.dot_general(sk, sk, (((0,), (0,)), ((), ())), preferred_element_type=F32)
        part_ref[...] += g.reshape(GROUP, 8, 128)

    pl.semaphore_wait(barrier, 2 * (GROUP - 1))

    def all_of(ref, sem):
        return pltpu.make_async_copy(ref.at[pl.ds(0, GROUP - 1)], ref.at[pl.ds(0, GROUP - 1)], sem)

    for d in range(1, GROUP):
        to = (ring + d) % GROUP
        pltpu.make_async_remote_copy(
            src_ref=part_ref.at[to], dst_ref=got1_ref.at[d - 1], send_sem=ar_put.at[0], recv_sem=ar_get.at[0],
            device_id=ring_peer(to), device_id_type=MESH).start()

    routes_copy.wait()
    masks = [jnp.int32(0)] * TILES
    for j in range(32):
        route = routes_ref[0, j]
        bit = (1 << j) if j < 31 else -(1 << 31)
        masks = [jnp.where(route == o, m | jnp.int32(bit), m) for o, m in enumerate(masks)]
    for o in range(TILES):
        m = masks[o]
        for k in range(SEND):
            low = m & (-m)
            table_ref[o, k] = jnp.where(m != 0, 31 - lax.clz(low), -1)
            m = m & (m - 1)

    def pick(o, k):
        at = table_ref[o, k]
        block = sk_ref[jnp.maximum(at, 0)]
        return jnp.where(at >= 0, block, jnp.zeros_like(block))

    parts = [part for step in START for part in step]

    def transfer(d, first, count):
        at = parts.index((d, first, count))
        return pltpu.make_async_remote_copy(
            src_ref=send_ref.at[d - 1, pl.ds(first, count)],
            dst_ref=placed_ref.at[tile, pl.ds(first, count)],
            send_sem=put_sem.at[at],
            recv_sem=get_sem.at[at],
            device_id=(slab, (tile + d) % TILES),
            device_id_type=MESH,
        )

    def fill(d, first, count):
        @pl.loop(first, first + count)
        def _(k):
            send_ref[d - 1, k] = pick((tile + d) % TILES, k)

    for part in START[0]:
        fill(*part)
        transfer(*part).start()
    for part in parts[len(START[0]):]:
        fill(*part)

    @pl.loop(0, SEND)
    def _(k):
        placed_ref[tile, k] = pick(tile, k)

    all_of(got1_ref, ar_get.at[0]).wait()
    mine = part_ref[ring]
    for d in range(GROUP - 1):
        mine = mine + got1_ref[d]
    got2_ref[face] = mine
    for d in range(1, GROUP):
        to = (face + d) % GROUP
        pltpu.make_async_remote_copy(
            src_ref=got2_ref.at[face], dst_ref=got2_ref.at[face], send_sem=ar_put.at[1], recv_sem=ar_get.at[1],
            device_id=face_peer(to), device_id_type=MESH).start()
    for part in START[1]:
        transfer(*part).start()
    all_of(got2_ref, ar_get.at[1]).wait()
    total = got2_ref[0]
    for d in range(1, GROUP):
        total = total + got2_ref[d]
    gram_ref[ring] = total
    for d in range(1, GROUP):
        to = (ring + d) % GROUP
        pltpu.make_async_remote_copy(
            src_ref=gram_ref.at[ring], dst_ref=gram_ref.at[ring], send_sem=ar_put.at[2], recv_sem=ar_get.at[2],
            device_id=ring_peer(to), device_id_type=MESH).start()
    for part in START[2]:
        transfer(*part).start()
    all_of(gram_ref, ar_get.at[2]).wait()

    factor(gram_ref, upper_ref, inverse_ref, work_ref)

    for i in range(3):
        all_of(got1_ref, ar_put.at[i]).wait()
    for part in parts:
        transfer(*part).wait()


def scale(cell_root, placed_ref, upper_ref, inverse_ref, basis_hbm, triangle_hbm, basis_ref, triangle_ref, sem, tri_sem):
    row = lax.broadcasted_iota(jnp.int32, (128, 128), 0)
    col = lax.broadcasted_iota(jnp.int32, (128, 128), 1)
    triangle_ref[...] = jnp.where(row <= col, upper_ref[...] * (1.0 / cell_root), 0.0)
    tri = pltpu.make_async_copy(triangle_ref, triangle_hbm, tri_sem)
    tri.start()
    h, m, l = split3(jnp.where(row >= col, inverse_ref[...] * cell_root, 0.0))
    count = placed_ref.shape[0] // STEPS

    def copy(i):
        part = pl.ds(i * count, count)
        return pltpu.make_async_copy(basis_ref.at[part], basis_hbm.at[part], sem.at[i])

    for i in range(STEPS):
        part = pl.ds(i * count, count)
        rows = placed_ref[part].reshape(count * 128, 128)
        out = sum(lax.dot_general(rows, w, (((1,), (1,)), ((), ())), preferred_element_type=F32) for w in (l, m, h))
        basis_ref[part] = out.astype(BF16).reshape(count, 128, 128)
        copy(i).start()
    tri.wait()
    for i in range(STEPS):
        copy(i).wait()


def local(snapshots, routes, sketch_matrix):
    cell_root = math.sqrt(snapshots.shape[0] * 128 * lax.axis_size("slab") * lax.axis_size("tile"))
    vmem = pl.BlockSpec(memory_space=pltpu.VMEM)
    hbm = pl.BlockSpec(memory_space=pltpu.HBM)
    square = jax.ShapeDtypeStruct((128, 128), F32)
    placed, upper, inverse = pl.pallas_call(
        exchange,
        out_shape=(jax.ShapeDtypeStruct((TILES, SEND, 128, 128), BF16), square, square),
        in_specs=[hbm, hbm, hbm],
        out_specs=(vmem, vmem, vmem),
        scratch_shapes=[
            pltpu.VMEM((32, 128, 256), BF16),
            pltpu.VMEM((256, 128), BF16),
            pltpu.SMEM((1, 32), jnp.int32),
            pltpu.VMEM((32, 128, 128), BF16),
            pltpu.VMEM((TILES - 1, SEND, 128, 128), BF16),
            pltpu.VMEM((GROUP, 8, 128), F32),
            pltpu.VMEM((GROUP, 8, 128), F32),
            pltpu.VMEM((GROUP, 8, 128), F32),
            pltpu.VMEM((GROUP, 8, 128), F32),
            pltpu.VMEM((128, 256), F32),
            pltpu.SMEM((TILES, SEND), jnp.int32),
            pltpu.SemaphoreType.DMA((PIECES,)),
            pltpu.SemaphoreType.DMA((2,)),
            pltpu.SemaphoreType.DMA((sum(map(len, START)),)),
            pltpu.SemaphoreType.DMA((sum(map(len, START)),)),
            pltpu.SemaphoreType.DMA((3,)),
            pltpu.SemaphoreType.DMA((3,)),
        ],
        compiler_params=pltpu.CompilerParams(collective_id=0, has_side_effects=True, vmem_limit_bytes=32 * 2**20),
        name="exchange",
    )(*(pltpu.with_memory_space_constraint(v, pltpu.HBM) for v in (routes.reshape(1, 32), snapshots, sketch_matrix)))
    return tuple(pl.pallas_call(
        lambda *refs: scale(cell_root, *refs),
        out_shape=(jax.ShapeDtypeStruct((TILES * SEND, 128, 128), BF16), square),
        in_specs=[vmem, vmem, vmem],
        out_specs=(hbm, hbm),
        scratch_shapes=[
            pltpu.VMEM((TILES * SEND, 128, 128), BF16),
            pltpu.VMEM((128, 128), F32),
            pltpu.SemaphoreType.DMA((STEPS,)),
            pltpu.SemaphoreType.DMA,
        ],
        compiler_params=pltpu.CompilerParams(vmem_limit_bytes=32 * 2**20),
        name="scale",
    )(placed.reshape(TILES * SEND, 128, 128), upper, inverse))


def solution(mesh):
    return jax.shard_map(
        local,
        mesh=mesh,
        in_specs=(P(("slab", "tile"), None, None), P(("slab", "tile"), None), P()),
        out_specs=(P(("slab", "tile"), None, None), P()),
        check_vma=False,
    )
```

```python
import math

import jax
import jax.numpy as jnp
from jax import lax
from jax.experimental import pallas as pl
from jax.experimental.pallas import tpu as pltpu
from jax.sharding import PartitionSpec as P

SEND = 10
TILES = 4
GROUP = 16
STEPS = 8
SPAN = 64
START = (((2, 0, 8),), (), ((2, 8, 2), (1, 0, 10), (3, 0, 10)), ())
RING = sorted(((dz, dc) for dz in range(8) for dc in range(2) if dz or dc), key=lambda d: -2 * min(d[0], 8 - d[0]) - d[1])
FACE = sorted(((dy, dx) for dy in range(4) for dx in range(4) if dy or dx), key=lambda d: -sum(min(v, 4 - v) for v in d))
MESH = pl.DeviceIdType.MESH
F32, BF16 = jnp.float32, jnp.bfloat16


def split3(v):
    h = v.astype(BF16)
    rest = v - h.astype(F32)
    m = rest.astype(BF16)
    return h, m, (rest - m.astype(F32)).astype(BF16)


def outer_products(u):
    h, m, l = split3(u)
    left = jnp.concatenate([v[:, :128] for v in (h, h, m, h, l, m)], 0)
    right = jnp.concatenate([h, m, h, l, h, m], 0)
    return lax.dot_general(left, right, (((0,), (0,)), ((), ())), preferred_element_type=F32)


def line(v, i):
    return jnp.broadcast_to(v[i : i + 1], (8, v.shape[1]))


def columns(rows, p):
    return [jnp.broadcast_to(rows[:, p + k : p + k + 1], (8, 128)) for k in range(8)]


def wide(v):
    return jnp.concatenate([v, v], 1)


def factor(gram_ref, upper_ref, inverse_ref, work):
    row = lax.broadcasted_iota(jnp.int32, (128, 128), 0)
    col = lax.broadcasted_iota(jnp.int32, (128, 128), 1)
    work[:, :128] = gram_ref[...].reshape(128, 128)
    work[:, 128:] = (row == col).astype(F32)
    sub = lax.broadcasted_iota(jnp.int32, (8, 256), 0)
    for s in range(0, 128, SPAN):
        rows = {q: work[q : q + 8, :] for q in range(s, s + SPAN, 8)}
        own = columns(rows[s], s)
        done = []
        for p in range(s, s + SPAN, 8):
            later = range(p + 8, s + SPAN, 8)
            cols = {q: columns(rows[q], p) for q in later}
            e = {(i, k): line(own[k], i) for k in range(8) for i in range(k, 8)}
            own = columns(rows[p + 8], p + 8) if later else None
            x = [line(rows[p], i) for i in range(8)]
            for k in range(8):
                r = lax.rsqrt(e[k, k])
                l = {i: e[i, k] * r for i in range(k + 1, 8)}
                for i in range(k + 1, 8):
                    for j in range(k + 1, i + 1):
                        e[i, j] = e[i, j] - l[i] * l[j]
                x[k] = x[k] * wide(r)
                for i in range(k + 1, 8):
                    x[i] = x[i] - wide(l[i]) * x[k]
                for q in later:
                    m = cols[q][k] * r
                    if q == p + 8:
                        own = [o - m * line(m, j) for j, o in enumerate(own)]
                    for j in range(k + 1, 8):
                        cols[q][j] = cols[q][j] - m * l[j]
                    rows[q] = rows[q] - wide(m) * x[k]
            u = x[0]
            for k in range(1, 8):
                u = jnp.where(sub == k, x[k], u)
            upper_ref[p : p + 8, :] = u[:, :128]
            inverse_ref[p : p + 8, :] = u[:, 128:]
            done.append(u)
        if s + SPAN < 128:
            g = outer_products(jnp.concatenate(done, 0))
            work[s + SPAN :, :] = work[s + SPAN :, :] - g[s + SPAN :, :]


def total_of(terms):
    while len(terms) > 1:
        terms = [sum(terms[i : i + 2]) for i in range(0, len(terms), 2)]
    return terms[0]


def exchange(routes_hbm, x_hbm, s_hbm, placed_ref, upper_ref, inverse_ref, x_ref, s_ref, routes_ref, sk_ref, send_ref, part_ref,
             got1_ref, got2_ref, gram_ref, work_ref, table_ref, in_sem, put_sem, get_sem, ar_put, ar_get):
    slab, tile = lax.axis_index("slab"), lax.axis_index("tile")
    core, y, z = slab % 2, (slab // 2) % 4, slab // 8
    ring = z * 2 + core
    face = y * 4 + tile

    ring_peers = []
    for dz, dc in RING:
        to_z, to_core = lax.rem(z + dz, 8), lax.rem(core + dc, 2)
        ring_peers.append((to_z * 2 + to_core, ((to_z * 4 + y) * 2 + to_core, tile)))
    face_peers = []
    for dy, dx in FACE:
        to_y, to_x = lax.rem(y + dy, 4), lax.rem(tile + dx, 4)
        face_peers.append((to_y * 4 + to_x, ((z * 4 + to_y) * 2 + core, to_x)))

    barrier = pltpu.get_barrier_semaphore()
    for _, peer in ring_peers + face_peers:
        pl.semaphore_signal(barrier, inc=1, device_id=peer, device_id_type=MESH)

    x_copy = pltpu.make_async_copy(x_hbm, x_ref, in_sem.at[0])
    s_copy = pltpu.make_async_copy(s_hbm, s_ref, in_sem.at[1])
    routes_copy = pltpu.make_async_copy(routes_hbm, routes_ref, in_sem.at[2])
    routes_copy.start()
    s_copy.start()
    x_copy.start()

    routes_copy.wait()
    masks = [jnp.int32(0)] * TILES
    for j in range(32):
        route = routes_ref[0, j]
        bit = (1 << j) if j < 31 else -(1 << 31)
        masks = [jnp.where(route == o, m | jnp.int32(bit), m) for o, m in enumerate(masks)]
    for o in range(TILES):
        m = masks[o]
        for k in range(SEND):
            low = m & (-m)
            table_ref[o, k] = jnp.where(m != 0, 31 - lax.clz(low), -1)
            m = m & (m - 1)

    s_copy.wait()
    x_copy.wait()
    cells = x_ref.shape[0] * 128
    sk = jnp.dot(x_ref[...].reshape(cells, 256), s_ref[...], preferred_element_type=F32).astype(BF16)
    sk_ref[...] = sk.reshape(sk_ref.shape)

    def all_of(ref, sem):
        return pltpu.make_async_copy(ref.at[pl.ds(0, GROUP - 1)], ref.at[pl.ds(0, GROUP - 1)], sem)

    def pick(o, k):
        at = table_ref[o, k]
        block = sk_ref[jnp.maximum(at, 0)]
        return jnp.where(at >= 0, block, jnp.zeros_like(block))

    parts = [part for step in START for part in step]

    def transfer(d, first, count):
        at = parts.index((d, first, count))
        return pltpu.make_async_remote_copy(
            src_ref=send_ref.at[d - 1, pl.ds(first, count)],
            dst_ref=placed_ref.at[tile, pl.ds(first, count)],
            send_sem=put_sem.at[at],
            recv_sem=get_sem.at[at],
            device_id=(slab, (tile + d) % TILES),
            device_id_type=MESH,
        )

    def fill(d, first, count):
        @pl.loop(first, first + count)
        def _(k):
            send_ref[d - 1, k] = pick((tile + d) % TILES, k)

    def begin(step):
        for part in START[step]:
            if step < 2:
                fill(*part)
            transfer(*part).start()

    pl.semaphore_wait(barrier, 2 * (GROUP - 1))
    begin(0)
    sk = sk_ref[...].reshape(cells, 128)
    gram = lax.dot_general(sk, sk, (((0,), (0,)), ((), ())), preferred_element_type=F32)
    part_ref[...] = gram.reshape(part_ref.shape)

    for i, (to, peer) in enumerate(ring_peers):
        pltpu.make_async_remote_copy(
            src_ref=part_ref.at[to], dst_ref=got1_ref.at[i], send_sem=ar_put.at[0], recv_sem=ar_get.at[0],
            device_id=peer, device_id_type=MESH).start()

    begin(1)
    for part in START[2] + START[3]:
        fill(*part)

    @pl.loop(0, SEND)
    def _(k):
        placed_ref[tile, k] = pick(tile, k)

    all_of(got1_ref, ar_get.at[0]).wait()
    got2_ref[face] = total_of([part_ref[ring]] + [got1_ref[i] for i in range(GROUP - 1)])
    for _, peer in face_peers:
        pltpu.make_async_remote_copy(
            src_ref=got2_ref.at[face], dst_ref=got2_ref.at[face], send_sem=ar_put.at[1], recv_sem=ar_get.at[1],
            device_id=peer, device_id_type=MESH).start()
    begin(2)
    all_of(got2_ref, ar_get.at[1]).wait()
    gram_ref[ring] = total_of([got2_ref[i] for i in range(GROUP)])
    for _, peer in ring_peers:
        pltpu.make_async_remote_copy(
            src_ref=gram_ref.at[ring], dst_ref=gram_ref.at[ring], send_sem=ar_put.at[2], recv_sem=ar_get.at[2],
            device_id=peer, device_id_type=MESH).start()
    begin(3)
    all_of(gram_ref, ar_get.at[2]).wait()

    factor(gram_ref, upper_ref, inverse_ref, work_ref)

    for i in range(3):
        all_of(got1_ref, ar_put.at[i]).wait()
    for part in parts:
        transfer(*part).wait()


def scale(cell_root, placed_ref, upper_ref, inverse_ref, basis_hbm, triangle_hbm, basis_ref, triangle_ref, sem, tri_sem):
    row = lax.broadcasted_iota(jnp.int32, (128, 128), 0)
    col = lax.broadcasted_iota(jnp.int32, (128, 128), 1)
    triangle_ref[...] = jnp.where(row <= col, upper_ref[...] * (1.0 / cell_root), 0.0)
    tri = pltpu.make_async_copy(triangle_ref, triangle_hbm, tri_sem)
    tri.start()
    h, m, _ = split3(jnp.where(row >= col, inverse_ref[...] * cell_root, 0.0))
    count = placed_ref.shape[0] // STEPS

    def copy(i):
        part = pl.ds(i * count, count)
        return pltpu.make_async_copy(basis_ref.at[part], basis_hbm.at[part], sem.at[i])

    for i in range(STEPS):
        part = pl.ds(i * count, count)
        rows = placed_ref[part].reshape(count * 128, 128)
        out = sum(lax.dot_general(rows, w, (((1,), (1,)), ((), ())), preferred_element_type=F32) for w in (m, h))
        basis_ref[part] = out.astype(BF16).reshape(count, 128, 128)
        copy(i).start()
    tri.wait()
    for i in range(STEPS):
        copy(i).wait()


def local(snapshots, routes, sketch_matrix):
    cell_root = math.sqrt(snapshots.shape[0] * 128 * lax.axis_size("slab") * lax.axis_size("tile"))
    vmem = pl.BlockSpec(memory_space=pltpu.VMEM)
    hbm = pl.BlockSpec(memory_space=pltpu.HBM)
    square = jax.ShapeDtypeStruct((128, 128), F32)
    placed, upper, inverse = pl.pallas_call(
        exchange,
        out_shape=(jax.ShapeDtypeStruct((TILES, SEND, 128, 128), BF16), square, square),
        in_specs=[hbm, hbm, hbm],
        out_specs=(vmem, vmem, vmem),
        scratch_shapes=[
            pltpu.VMEM((32, 128, 256), BF16),
            pltpu.VMEM((256, 128), BF16),
            pltpu.SMEM((1, 32), jnp.int32),
            pltpu.VMEM((32, 128, 128), BF16),
            pltpu.VMEM((TILES - 1, SEND, 128, 128), BF16),
            pltpu.VMEM((GROUP, 8, 128), F32),
            pltpu.VMEM((GROUP, 8, 128), F32),
            pltpu.VMEM((GROUP, 8, 128), F32),
            pltpu.VMEM((GROUP, 8, 128), F32),
            pltpu.VMEM((128, 256), F32),
            pltpu.SMEM((TILES, SEND), jnp.int32),
            pltpu.SemaphoreType.DMA((3,)),
            pltpu.SemaphoreType.DMA((sum(map(len, START)),)),
            pltpu.SemaphoreType.DMA((sum(map(len, START)),)),
            pltpu.SemaphoreType.DMA((3,)),
            pltpu.SemaphoreType.DMA((3,)),
        ],
        compiler_params=pltpu.CompilerParams(collective_id=0, has_side_effects=True, vmem_limit_bytes=32 * 2**20),
        name="exchange",
    )(*(pltpu.with_memory_space_constraint(v, pltpu.HBM) for v in (routes.reshape(1, 32), snapshots, sketch_matrix)))
    return tuple(pl.pallas_call(
        lambda *refs: scale(cell_root, *refs),
        out_shape=(jax.ShapeDtypeStruct((TILES * SEND, 128, 128), BF16), square),
        in_specs=[vmem, vmem, vmem],
        out_specs=(hbm, hbm),
        scratch_shapes=[
            pltpu.VMEM((TILES * SEND, 128, 128), BF16),
            pltpu.VMEM((128, 128), F32),
            pltpu.SemaphoreType.DMA((STEPS,)),
            pltpu.SemaphoreType.DMA,
        ],
        compiler_params=pltpu.CompilerParams(vmem_limit_bytes=32 * 2**20),
        name="scale",
    )(placed.reshape(TILES * SEND, 128, 128), upper, inverse))


def solution(mesh):
    return jax.shard_map(
        local,
        mesh=mesh,
        in_specs=(P(("slab", "tile"), None, None), P(("slab", "tile"), None), P()),
        out_specs=(P(("slab", "tile"), None, None), P()),
        check_vma=False,
    )
```

```python
import math

import jax
import jax.numpy as jnp
from jax import lax
from jax.experimental import pallas as pl
from jax.experimental.pallas import tpu as pltpu
from jax.sharding import PartitionSpec as P

SEND = 10
TILES = 4
GROUP = 16
STEPS = 8
SPAN = 64
START = (((2, 0, 6),), ((1, 0, 10), (3, 0, 10)), ((2, 6, 4),))
RING = sorted(((dz, dc) for dz in range(8) for dc in range(2) if dz or dc), key=lambda d: -2 * min(d[0], 8 - d[0]) - d[1])
FACE = sorted(((dy, dx) for dy in range(4) for dx in range(4) if dy or dx), key=lambda d: -sum(min(v, 4 - v) for v in d))
MESH = pl.DeviceIdType.MESH
F32, BF16 = jnp.float32, jnp.bfloat16


def split3(v):
    h = v.astype(BF16)
    rest = v - h.astype(F32)
    m = rest.astype(BF16)
    return h, m, (rest - m.astype(F32)).astype(BF16)


def outer_products(u):
    h, m, l = split3(u)
    left = jnp.concatenate([v[:, :128] for v in (h, h, m, h, l, m)], 0)
    right = jnp.concatenate([h, m, h, l, h, m], 0)
    return lax.dot_general(left, right, (((0,), (0,)), ((), ())), preferred_element_type=F32)


def line(v, i):
    return jnp.broadcast_to(v[i : i + 1], (8, v.shape[1]))


def columns(rows, p):
    return [jnp.broadcast_to(rows[:, p + k : p + k + 1], (8, 128)) for k in range(8)]


def wide(v):
    return jnp.concatenate([v, v], 1)


def factor(gram_ref, upper_ref, inverse_ref, work):
    row = lax.broadcasted_iota(jnp.int32, (128, 128), 0)
    col = lax.broadcasted_iota(jnp.int32, (128, 128), 1)
    work[:, :128] = gram_ref[...].reshape(128, 128)
    work[:, 128:] = (row == col).astype(F32)
    sub = lax.broadcasted_iota(jnp.int32, (8, 256), 0)
    for s in range(0, 128, SPAN):
        rows = {q: work[q : q + 8, :] for q in range(s, s + SPAN, 8)}
        own = columns(rows[s], s)
        done = []
        for p in range(s, s + SPAN, 8):
            later = range(p + 8, s + SPAN, 8)
            cols = {q: columns(rows[q], p) for q in later}
            e = {(i, k): line(own[k], i) for k in range(8) for i in range(k, 8)}
            own = columns(rows[p + 8], p + 8) if later else None
            x = [line(rows[p], i) for i in range(8)]
            for k in range(8):
                r = lax.rsqrt(e[k, k])
                l = {i: e[i, k] * r for i in range(k + 1, 8)}
                for i in range(k + 1, 8):
                    for j in range(k + 1, i + 1):
                        e[i, j] = e[i, j] - l[i] * l[j]
                x[k] = x[k] * wide(r)
                for i in range(k + 1, 8):
                    x[i] = x[i] - wide(l[i]) * x[k]
                for q in later:
                    m = cols[q][k] * r
                    if q == p + 8:
                        own = [o - m * line(m, j) for j, o in enumerate(own)]
                    for j in range(k + 1, 8):
                        cols[q][j] = cols[q][j] - m * l[j]
                    rows[q] = rows[q] - wide(m) * x[k]
            u = x[0]
            for k in range(1, 8):
                u = jnp.where(sub == k, x[k], u)
            upper_ref[p : p + 8, :] = u[:, :128]
            inverse_ref[p : p + 8, :] = u[:, 128:]
            done.append(u)
        if s + SPAN < 128:
            g = outer_products(jnp.concatenate(done, 0))
            work[s + SPAN :, :] = work[s + SPAN :, :] - g[s + SPAN :, :]


def total_of(terms):
    while len(terms) > 1:
        terms = [sum(terms[i : i + 2]) for i in range(0, len(terms), 2)]
    return terms[0]


def exchange(routes_hbm, x_hbm, s_hbm, placed_ref, upper_ref, inverse_ref, x_ref, s_ref, routes_ref, sk_ref, send_ref, part_ref,
             got1_ref, got2_ref, gram_ref, work_ref, table_ref, in_sem, put_sem, get_sem, ar_put, ar_get):
    x_copy = pltpu.make_async_copy(x_hbm, x_ref, in_sem.at[0])
    s_copy = pltpu.make_async_copy(s_hbm, s_ref, in_sem.at[1])
    routes_copy = pltpu.make_async_copy(routes_hbm, routes_ref, in_sem.at[2])
    routes_copy.start()
    s_copy.start()
    x_copy.start()

    slab, tile = lax.axis_index("slab"), lax.axis_index("tile")
    core, y, z = slab % 2, (slab // 2) % 4, slab // 8
    ring = z * 2 + core
    face = y * 4 + tile

    ring_peers = []
    for dz, dc in RING:
        to_z, to_core = lax.rem(z + dz, 8), lax.rem(core + dc, 2)
        ring_peers.append((to_z * 2 + to_core, ((to_z * 4 + y) * 2 + to_core, tile)))
    face_peers = []
    for dy, dx in FACE:
        to_y, to_x = lax.rem(y + dy, 4), lax.rem(tile + dx, 4)
        face_peers.append((to_y * 4 + to_x, ((z * 4 + to_y) * 2 + core, to_x)))

    barrier = pltpu.get_barrier_semaphore()
    for _, peer in ring_peers + face_peers:
        pl.semaphore_signal(barrier, inc=1, device_id=peer, device_id_type=MESH)

    routes_copy.wait()
    masks = [jnp.int32(0)] * TILES
    for j in range(32):
        route = routes_ref[0, j]
        bit = (1 << j) if j < 31 else -(1 << 31)
        masks = [jnp.where(route == o, m | jnp.int32(bit), m) for o, m in enumerate(masks)]
    for o in range(TILES):
        m = masks[o]
        for k in range(SEND):
            low = m & (-m)
            table_ref[o, k] = jnp.where(m != 0, 31 - lax.clz(low), -1)
            m = m & (m - 1)

    s_copy.wait()
    x_copy.wait()
    cells = x_ref.shape[0] * 128
    sk = jnp.dot(x_ref[...].reshape(cells, 256), s_ref[...], preferred_element_type=F32).astype(BF16)
    sk_ref[...] = sk.reshape(sk_ref.shape)

    def all_of(ref, sem):
        return pltpu.make_async_copy(ref.at[pl.ds(0, GROUP - 1)], ref.at[pl.ds(0, GROUP - 1)], sem)

    def pick(o, k):
        at = table_ref[o, k]
        block = sk_ref[jnp.maximum(at, 0)]
        return jnp.where(at >= 0, block, jnp.zeros_like(block))

    parts = [part for step in START for part in step]

    def transfer(d, first, count):
        at = parts.index((d, first, count))
        return pltpu.make_async_remote_copy(
            src_ref=send_ref.at[d - 1, pl.ds(first, count)],
            dst_ref=placed_ref.at[tile, pl.ds(first, count)],
            send_sem=put_sem.at[at],
            recv_sem=get_sem.at[at],
            device_id=(slab, (tile + d) % TILES),
            device_id_type=MESH,
        )

    def fill(d, first, count):
        @pl.loop(first, first + count)
        def _(k):
            send_ref[d - 1, k] = pick((tile + d) % TILES, k)

    def begin(step):
        for part in START[step]:
            if step == 0:
                fill(*part)
            transfer(*part).start()

    gram = lax.dot_general(sk, sk, (((0,), (0,)), ((), ())), preferred_element_type=F32)
    part_ref[...] = gram.reshape(part_ref.shape)
    pl.semaphore_wait(barrier, 2 * (GROUP - 1))

    for i, (to, peer) in enumerate(ring_peers):
        pltpu.make_async_remote_copy(
            src_ref=part_ref.at[to], dst_ref=got1_ref.at[i], send_sem=ar_put.at[0], recv_sem=ar_get.at[0],
            device_id=peer, device_id_type=MESH).start()

    begin(0)
    for part in START[1] + START[2]:
        fill(*part)

    @pl.loop(0, SEND)
    def _(k):
        placed_ref[tile, k] = pick(tile, k)

    all_of(got1_ref, ar_get.at[0]).wait()
    got2_ref[face] = total_of([part_ref[ring]] + [got1_ref[i] for i in range(GROUP - 1)])
    for _, peer in face_peers:
        pltpu.make_async_remote_copy(
            src_ref=got2_ref.at[face], dst_ref=got2_ref.at[face], send_sem=ar_put.at[1], recv_sem=ar_get.at[1],
            device_id=peer, device_id_type=MESH).start()
    begin(1)
    all_of(got2_ref, ar_get.at[1]).wait()
    gram_ref[ring] = total_of([got2_ref[i] for i in range(GROUP)])
    for _, peer in ring_peers:
        pltpu.make_async_remote_copy(
            src_ref=gram_ref.at[ring], dst_ref=gram_ref.at[ring], send_sem=ar_put.at[2], recv_sem=ar_get.at[2],
            device_id=peer, device_id_type=MESH).start()
    begin(2)
    all_of(gram_ref, ar_get.at[2]).wait()

    factor(gram_ref, upper_ref, inverse_ref, work_ref)

    for i in range(3):
        all_of(got1_ref, ar_put.at[i]).wait()
    for part in parts:
        transfer(*part).wait()


def scale(cell_root, placed_ref, upper_ref, inverse_ref, basis_hbm, triangle_hbm, basis_ref, triangle_ref, sem, tri_sem):
    row = lax.broadcasted_iota(jnp.int32, (128, 128), 0)
    col = lax.broadcasted_iota(jnp.int32, (128, 128), 1)
    triangle_ref[...] = jnp.where(row <= col, upper_ref[...] * (1.0 / cell_root), 0.0)
    tri = pltpu.make_async_copy(triangle_ref, triangle_hbm, tri_sem)
    tri.start()
    h, m, _ = split3(jnp.where(row >= col, inverse_ref[...] * cell_root, 0.0))
    count = placed_ref.shape[0] // STEPS

    def copy(i):
        part = pl.ds(i * count, count)
        return pltpu.make_async_copy(basis_ref.at[part], basis_hbm.at[part], sem.at[i])

    for i in range(STEPS):
        part = pl.ds(i * count, count)
        rows = placed_ref[part].reshape(count * 128, 128)
        out = sum(lax.dot_general(rows, w, (((1,), (1,)), ((), ())), preferred_element_type=F32) for w in (m, h))
        basis_ref[part] = out.astype(BF16).reshape(count, 128, 128)
        copy(i).start()
    tri.wait()
    for i in range(STEPS):
        copy(i).wait()


def local(snapshots, routes, sketch_matrix):
    cell_root = math.sqrt(snapshots.shape[0] * 128 * lax.axis_size("slab") * lax.axis_size("tile"))
    vmem = pl.BlockSpec(memory_space=pltpu.VMEM)
    hbm = pl.BlockSpec(memory_space=pltpu.HBM)
    square = jax.ShapeDtypeStruct((128, 128), F32)
    placed, upper, inverse = pl.pallas_call(
        exchange,
        out_shape=(jax.ShapeDtypeStruct((TILES, SEND, 128, 128), BF16), square, square),
        in_specs=[hbm, hbm, hbm],
        out_specs=(vmem, vmem, vmem),
        scratch_shapes=[
            pltpu.VMEM((32, 128, 256), BF16),
            pltpu.VMEM((256, 128), BF16),
            pltpu.SMEM((1, 32), jnp.int32),
            pltpu.VMEM((32, 128, 128), BF16),
            pltpu.VMEM((TILES - 1, SEND, 128, 128), BF16),
            pltpu.VMEM((GROUP, 8, 128), F32),
            pltpu.VMEM((GROUP, 8, 128), F32),
            pltpu.VMEM((GROUP, 8, 128), F32),
            pltpu.VMEM((GROUP, 8, 128), F32),
            pltpu.VMEM((128, 256), F32),
            pltpu.SMEM((TILES, SEND), jnp.int32),
            pltpu.SemaphoreType.DMA((3,)),
            pltpu.SemaphoreType.DMA((sum(map(len, START)),)),
            pltpu.SemaphoreType.DMA((sum(map(len, START)),)),
            pltpu.SemaphoreType.DMA((3,)),
            pltpu.SemaphoreType.DMA((3,)),
        ],
        compiler_params=pltpu.CompilerParams(collective_id=0, has_side_effects=True, vmem_limit_bytes=32 * 2**20),
        name="exchange",
    )(*(pltpu.with_memory_space_constraint(v, pltpu.HBM) for v in (routes.reshape(1, 32), snapshots, sketch_matrix)))
    return tuple(pl.pallas_call(
        lambda *refs: scale(cell_root, *refs),
        out_shape=(jax.ShapeDtypeStruct((TILES * SEND, 128, 128), BF16), square),
        in_specs=[vmem, vmem, vmem],
        out_specs=(hbm, hbm),
        scratch_shapes=[
            pltpu.VMEM((TILES * SEND, 128, 128), BF16),
            pltpu.VMEM((128, 128), F32),
            pltpu.SemaphoreType.DMA((STEPS,)),
            pltpu.SemaphoreType.DMA,
        ],
        compiler_params=pltpu.CompilerParams(vmem_limit_bytes=32 * 2**20),
        name="scale",
    )(placed.reshape(TILES * SEND, 128, 128), upper, inverse))


def solution(mesh):
    return jax.shard_map(
        local,
        mesh=mesh,
        in_specs=(P(("slab", "tile"), None, None), P(("slab", "tile"), None), P()),
        out_specs=(P(("slab", "tile"), None, None), P()),
        check_vma=False,
    )
```

```python
import math

import jax
import jax.numpy as jnp
from jax import lax
from jax.experimental import pallas as pl
from jax.experimental.pallas import tpu as pltpu
from jax.sharding import PartitionSpec as P

SEND = 10
TILES = 4
GROUP = 16
STEPS = 8
SPAN = 64
START = (((2, 0, 7),), ((1, 0, 10), (3, 0, 10)), ((2, 7, 3),))
RING = sorted(((dz, dc) for dz in range(8) for dc in range(2) if dz or dc), key=lambda d: -2 * min(d[0], 8 - d[0]) - d[1])
FACE = sorted(((dy, dx) for dy in range(4) for dx in range(4) if dy or dx), key=lambda d: -sum(min(v, 4 - v) for v in d))
MESH = pl.DeviceIdType.MESH
F32, BF16 = jnp.float32, jnp.bfloat16


def split3(v):
    h = v.astype(BF16)
    rest = v - h.astype(F32)
    m = rest.astype(BF16)
    return h, m, (rest - m.astype(F32)).astype(BF16)


def outer_products(u):
    h, m, l = split3(u)
    left = jnp.concatenate([v[:, :128] for v in (h, h, m, h, l, m)], 0)
    right = jnp.concatenate([h, m, h, l, h, m], 0)
    return lax.dot_general(left, right, (((0,), (0,)), ((), ())), preferred_element_type=F32)


def line(v, i):
    return jnp.broadcast_to(v[i : i + 1], (8, v.shape[1]))


def columns(rows, p):
    return [jnp.broadcast_to(rows[:, p + k : p + k + 1], (8, 128)) for k in range(8)]


def wide(v):
    return jnp.concatenate([v, v], 1)


def factor(gram_ref, upper_ref, inverse_ref, arrive):
    row = lax.broadcasted_iota(jnp.int32, (8, 128), 0)
    col = lax.broadcasted_iota(jnp.int32, (8, 128), 1)
    sub = lax.broadcasted_iota(jnp.int32, (8, 256), 0)
    product = None
    for s in range(0, 128, SPAN):
        arrive(s // SPAN)
        rows = {q: jnp.concatenate([gram_ref[q // 8], (row + q == col).astype(F32)], 1) for q in range(s, s + SPAN, 8)}
        if s:
            rows = {q: v - product[q : q + 8] for q, v in rows.items()}
        own = columns(rows[s], s)
        done = []
        for p in range(s, s + SPAN, 8):
            later = range(p + 8, s + SPAN, 8)
            cols = {q: columns(rows[q], p) for q in later}
            e = {(i, k): line(own[k], i) for k in range(8) for i in range(k, 8)}
            own = columns(rows[p + 8], p + 8) if later else None
            x = [line(rows[p], i) for i in range(8)]
            for k in range(8):
                r = lax.rsqrt(e[k, k])
                l = {i: e[i, k] * r for i in range(k + 1, 8)}
                for i in range(k + 1, 8):
                    for j in range(k + 1, i + 1):
                        e[i, j] = e[i, j] - l[i] * l[j]
                x[k] = x[k] * wide(r)
                for i in range(k + 1, 8):
                    x[i] = x[i] - wide(l[i]) * x[k]
                for q in later:
                    m = cols[q][k] * r
                    if q == p + 8:
                        own = [o - m * line(m, j) for j, o in enumerate(own)]
                    for j in range(k + 1, 8):
                        cols[q][j] = cols[q][j] - m * l[j]
                    rows[q] = rows[q] - wide(m) * x[k]
            u = x[0]
            for k in range(1, 8):
                u = jnp.where(sub == k, x[k], u)
            upper_ref[p : p + 8, :] = u[:, :128]
            inverse_ref[p : p + 8, :] = u[:, 128:]
            done.append(u)
        if s + SPAN < 128:
            product = outer_products(jnp.concatenate(done, 0))


def total_of(terms):
    while len(terms) > 1:
        terms = [sum(terms[i : i + 2]) for i in range(0, len(terms), 2)]
    return terms[0]


def exchange(routes_hbm, x_hbm, s_hbm, placed_ref, upper_ref, inverse_ref, x_ref, s_ref, routes_ref, sk_ref, send_ref, part_ref,
             got1_ref, got2_ref, gram_ref, sum_ref, table_ref, in_sem, put_sem, get_sem, ar_put, ar_get, half_get):
    slab, tile = lax.axis_index("slab"), lax.axis_index("tile")
    core, y, z = slab % 2, (slab // 2) % 4, slab // 8
    ring = z * 2 + core
    face = y * 4 + tile

    barrier = pltpu.get_barrier_semaphore()
    ring_peers, face_peers = [], []
    for dz, dc in RING:
        to_z, to_core = lax.rem(z + dz, 8), lax.rem(core + dc, 2)
        ring_peers.append((to_z * 2 + to_core, ((to_z * 4 + y) * 2 + to_core, tile)))
        pl.semaphore_signal(barrier, inc=1, device_id=ring_peers[-1][1], device_id_type=MESH)
    x_copy = pltpu.make_async_copy(x_hbm, x_ref, in_sem.at[0])
    s_copy = pltpu.make_async_copy(s_hbm, s_ref, in_sem.at[1])
    routes_copy = pltpu.make_async_copy(routes_hbm, routes_ref, in_sem.at[2])
    routes_copy.start()
    s_copy.start()
    x_copy.start()
    for dy, dx in FACE:
        to_y, to_x = lax.rem(y + dy, 4), lax.rem(tile + dx, 4)
        face_peers.append((to_y * 4 + to_x, ((z * 4 + to_y) * 2 + core, to_x)))
        pl.semaphore_signal(barrier, inc=1, device_id=face_peers[-1][1], device_id_type=MESH)

    s_copy.wait()
    x_copy.wait()
    cells = x_ref.shape[0] * 128
    sk = jnp.dot(x_ref[...].reshape(cells, 256), s_ref[...], preferred_element_type=F32).astype(BF16)
    sk_ref[...] = sk.reshape(sk_ref.shape)

    def all_of(ref, sem):
        return pltpu.make_async_copy(ref.at[pl.ds(0, GROUP - 1)], ref.at[pl.ds(0, GROUP - 1)], sem)

    def pick(o, k):
        at = table_ref[o, k]
        block = sk_ref[jnp.maximum(at, 0)]
        return jnp.where(at >= 0, block, jnp.zeros_like(block))

    parts = [part for step in START for part in step]

    def transfer(d, first, count):
        at = parts.index((d, first, count))
        return pltpu.make_async_remote_copy(
            src_ref=send_ref.at[d - 1, pl.ds(first, count)],
            dst_ref=placed_ref.at[tile, pl.ds(first, count)],
            send_sem=put_sem.at[at],
            recv_sem=get_sem.at[at],
            device_id=(slab, (tile + d) % TILES),
            device_id_type=MESH,
        )

    def fill(d, first, count):
        @pl.loop(first, first + count)
        def _(k):
            send_ref[d - 1, k] = pick((tile + d) % TILES, k)

    def begin(step):
        for part in START[step]:
            if step == 0:
                fill(*part)
            transfer(*part).start()

    gram = lax.dot_general(sk, sk, (((0,), (0,)), ((), ())), preferred_element_type=F32)
    part_ref[...] = gram.reshape(part_ref.shape)
    pl.semaphore_wait(barrier, 2 * (GROUP - 1))

    for i, (to, peer) in enumerate(ring_peers):
        pltpu.make_async_remote_copy(
            src_ref=part_ref.at[to], dst_ref=got1_ref.at[i], send_sem=ar_put.at[0], recv_sem=ar_get.at[0],
            device_id=peer, device_id_type=MESH).start()

    routes_copy.wait()
    masks = [jnp.int32(0)] * TILES
    for j in range(32):
        route = routes_ref[0, j]
        bit = (1 << j) if j < 31 else -(1 << 31)
        masks = [jnp.where(route == o, m | jnp.int32(bit), m) for o, m in enumerate(masks)]
    for o in range(TILES):
        m = masks[o]
        for k in range(SEND):
            low = m & (-m)
            table_ref[o, k] = jnp.where(m != 0, 31 - lax.clz(low), -1)
            m = m & (m - 1)

    begin(0)
    for part in START[1] + START[2]:
        fill(*part)

    @pl.loop(0, SEND)
    def _(k):
        placed_ref[tile, k] = pick(tile, k)

    all_of(got1_ref, ar_get.at[0]).wait()
    got2_ref[face] = total_of([part_ref[ring]] + [got1_ref[i] for i in range(GROUP - 1)])
    for _, peer in face_peers:
        pltpu.make_async_remote_copy(
            src_ref=got2_ref.at[face], dst_ref=got2_ref.at[face], send_sem=ar_put.at[1], recv_sem=ar_get.at[1],
            device_id=peer, device_id_type=MESH).start()
    begin(1)
    all_of(got2_ref, ar_get.at[1]).wait()
    sum_ref[...] = total_of([got2_ref[i] for i in range(GROUP)])
    half = ring // (GROUP // 2)
    for _, peer in ring_peers:
        pltpu.make_async_remote_copy(
            src_ref=sum_ref, dst_ref=gram_ref.at[ring], send_sem=ar_put.at[2], recv_sem=half_get.at[half],
            device_id=peer, device_id_type=MESH).start()
    pltpu.make_async_copy(sum_ref, gram_ref.at[ring], half_get.at[half]).start()
    begin(2)

    def arrive(i):
        part = gram_ref.at[pl.ds(i * (GROUP // 2), GROUP // 2)]
        pltpu.make_async_copy(part, part, half_get.at[i]).wait()

    factor(gram_ref, upper_ref, inverse_ref, arrive)

    for i in range(3):
        all_of(got1_ref, ar_put.at[i]).wait()
    for part in parts:
        transfer(*part).wait()


def scale(cell_root, placed_ref, upper_ref, inverse_ref, basis_hbm, triangle_hbm, basis_ref, triangle_ref, sem, tri_sem):
    row = lax.broadcasted_iota(jnp.int32, (128, 128), 0)
    col = lax.broadcasted_iota(jnp.int32, (128, 128), 1)
    triangle_ref[...] = jnp.where(row <= col, upper_ref[...] * (1.0 / cell_root), 0.0)
    tri = pltpu.make_async_copy(triangle_ref, triangle_hbm, tri_sem)
    tri.start()
    h, m, _ = split3(jnp.where(row >= col, inverse_ref[...] * cell_root, 0.0))
    count = placed_ref.shape[0] // STEPS

    def copy(i):
        part = pl.ds(i * count, count)
        return pltpu.make_async_copy(basis_ref.at[part], basis_hbm.at[part], sem.at[i])

    for i in range(STEPS):
        part = pl.ds(i * count, count)
        rows = placed_ref[part].reshape(count * 128, 128)
        out = sum(lax.dot_general(rows, w, (((1,), (1,)), ((), ())), preferred_element_type=F32) for w in (m, h))
        basis_ref[part] = out.astype(BF16).reshape(count, 128, 128)
        copy(i).start()
    tri.wait()
    for i in range(STEPS):
        copy(i).wait()


def local(snapshots, routes, sketch_matrix):
    cell_root = math.sqrt(snapshots.shape[0] * 128 * lax.axis_size("slab") * lax.axis_size("tile"))
    vmem = pl.BlockSpec(memory_space=pltpu.VMEM)
    hbm = pl.BlockSpec(memory_space=pltpu.HBM)
    square = jax.ShapeDtypeStruct((128, 128), F32)
    placed, upper, inverse = pl.pallas_call(
        exchange,
        out_shape=(jax.ShapeDtypeStruct((TILES, SEND, 128, 128), BF16), square, square),
        in_specs=[hbm, hbm, hbm],
        out_specs=(vmem, vmem, vmem),
        scratch_shapes=[
            pltpu.VMEM((32, 128, 256), BF16),
            pltpu.VMEM((256, 128), BF16),
            pltpu.SMEM((1, 32), jnp.int32),
            pltpu.VMEM((32, 128, 128), BF16),
            pltpu.VMEM((TILES - 1, SEND, 128, 128), BF16),
            pltpu.VMEM((GROUP, 8, 128), F32),
            pltpu.VMEM((GROUP, 8, 128), F32),
            pltpu.VMEM((GROUP, 8, 128), F32),
            pltpu.VMEM((GROUP, 8, 128), F32),
            pltpu.VMEM((8, 128), F32),
            pltpu.SMEM((TILES, SEND), jnp.int32),
            pltpu.SemaphoreType.DMA((3,)),
            pltpu.SemaphoreType.DMA((sum(map(len, START)),)),
            pltpu.SemaphoreType.DMA((sum(map(len, START)),)),
            pltpu.SemaphoreType.DMA((3,)),
            pltpu.SemaphoreType.DMA((2,)),
            pltpu.SemaphoreType.DMA((2,)),
        ],
        compiler_params=pltpu.CompilerParams(collective_id=0, has_side_effects=True, vmem_limit_bytes=32 * 2**20),
        name="exchange",
    )(*(pltpu.with_memory_space_constraint(v, pltpu.HBM) for v in (routes.reshape(1, 32), snapshots, sketch_matrix)))
    return tuple(pl.pallas_call(
        lambda *refs: scale(cell_root, *refs),
        out_shape=(jax.ShapeDtypeStruct((TILES * SEND, 128, 128), BF16), square),
        in_specs=[vmem, vmem, vmem],
        out_specs=(hbm, hbm),
        scratch_shapes=[
            pltpu.VMEM((TILES * SEND, 128, 128), BF16),
            pltpu.VMEM((128, 128), F32),
            pltpu.SemaphoreType.DMA((STEPS,)),
            pltpu.SemaphoreType.DMA,
        ],
        compiler_params=pltpu.CompilerParams(vmem_limit_bytes=32 * 2**20),
        name="scale",
    )(placed.reshape(TILES * SEND, 128, 128), upper, inverse))


def solution(mesh):
    return jax.shard_map(
        local,
        mesh=mesh,
        in_specs=(P(("slab", "tile"), None, None), P(("slab", "tile"), None), P()),
        out_specs=(P(("slab", "tile"), None, None), P()),
        check_vma=False,
    )
```

```python
import math

import jax
import jax.numpy as jnp
from jax import lax
from jax.experimental import pallas as pl
from jax.experimental.pallas import tpu as pltpu
from jax.sharding import PartitionSpec as P

SEND = 10
TILES = 4
GROUP = 16
STEPS = 8
SPAN = 64
START = (((2, 0, 7),), ((1, 0, 10), (3, 0, 10)), ((2, 7, 3),))
RING = sorted(((dz, dc) for dz in range(8) for dc in range(2) if dz or dc), key=lambda d: -2 * min(d[0], 8 - d[0]) - d[1])
FACE = sorted(((dy, dx) for dy in range(4) for dx in range(4) if dy or dx), key=lambda d: -sum(min(v, 4 - v) for v in d))
MESH = pl.DeviceIdType.MESH
F32, BF16 = jnp.float32, jnp.bfloat16


def split3(v):
    h = v.astype(BF16)
    rest = v - h.astype(F32)
    m = rest.astype(BF16)
    return h, m, (rest - m.astype(F32)).astype(BF16)


def outer_products(u):
    h, m, l = split3(u)
    left = jnp.concatenate([v[:, :128] for v in (h, h, m, h, l, m)], 0)
    right = jnp.concatenate([h, m, h, l, h, m], 0)
    return lax.dot_general(left, right, (((0,), (0,)), ((), ())), preferred_element_type=F32)


def line(v, i):
    return jnp.broadcast_to(v[i : i + 1], (8, v.shape[1]))


def columns(rows, p):
    return [jnp.broadcast_to(rows[:, p + k : p + k + 1], (8, 128)) for k in range(8)]


def wide(v):
    return jnp.concatenate([v, v], 1)


def factor(gram_ref, upper_ref, inverse_ref, arrive):
    row = lax.broadcasted_iota(jnp.int32, (8, 128), 0)
    col = lax.broadcasted_iota(jnp.int32, (8, 128), 1)
    sub = lax.broadcasted_iota(jnp.int32, (8, 256), 0)
    product = None
    for s in range(0, 128, SPAN):
        arrive(s // SPAN)
        rows = {q: jnp.concatenate([gram_ref[q // 8], (row + q == col).astype(F32)], 1) for q in range(s, s + SPAN, 8)}
        if s:
            rows = {q: v - product[q : q + 8] for q, v in rows.items()}
        own = columns(rows[s], s)
        done = []
        for p in range(s, s + SPAN, 8):
            later = range(p + 8, s + SPAN, 8)
            cols = {q: columns(rows[q], p) for q in later}
            e = {(i, k): line(own[k], i) for k in range(8) for i in range(k, 8)}
            own = columns(rows[p + 8], p + 8) if later else None
            x = [line(rows[p], i) for i in range(8)]
            for k in range(8):
                r = lax.rsqrt(e[k, k])
                l = {i: e[i, k] * r for i in range(k + 1, 8)}
                for i in range(k + 1, 8):
                    for j in range(k + 1, i + 1):
                        e[i, j] = e[i, j] - l[i] * l[j]
                x[k] = x[k] * wide(r)
                for i in range(k + 1, 8):
                    x[i] = x[i] - wide(l[i]) * x[k]
                for q in later:
                    m = cols[q][k] * r
                    if q == p + 8:
                        own = [o - m * line(m, j) for j, o in enumerate(own)]
                    for j in range(k + 1, 8):
                        cols[q][j] = cols[q][j] - m * l[j]
                    rows[q] = rows[q] - wide(m) * x[k]
            u = x[0]
            for k in range(1, 8):
                u = jnp.where(sub == k, x[k], u)
            upper_ref[p : p + 8, :] = u[:, :128]
            inverse_ref[p : p + 8, :] = u[:, 128:]
            done.append(u)
        if s + SPAN < 128:
            product = outer_products(jnp.concatenate(done, 0))


def total_of(terms):
    while len(terms) > 1:
        terms = [sum(terms[i : i + 2]) for i in range(0, len(terms), 2)]
    return terms[0]


def exchange(routes_hbm, x_hbm, s_hbm, placed_ref, upper_ref, inverse_ref, x_ref, s_ref, routes_ref, sk_ref, send_ref, part_ref,
             got1_ref, got2_ref, gram_ref, sum_ref, table_ref, in_sem, put_sem, get_sem, ar_put, ar_get, half_get):
    slab, tile = lax.axis_index("slab"), lax.axis_index("tile")
    core, y, z = slab % 2, (slab // 2) % 4, slab // 8
    ring = z * 2 + core
    face = y * 4 + tile

    barrier = pltpu.get_barrier_semaphore()
    ring_peers, face_peers = [], []
    for dz, dc in RING:
        to_z, to_core = lax.rem(z + dz, 8), lax.rem(core + dc, 2)
        ring_peers.append((to_z * 2 + to_core, ((to_z * 4 + y) * 2 + to_core, tile)))
        pl.semaphore_signal(barrier, inc=1, device_id=ring_peers[-1][1], device_id_type=MESH)
    x_copy = pltpu.make_async_copy(x_hbm, x_ref, in_sem.at[0])
    s_copy = pltpu.make_async_copy(s_hbm, s_ref, in_sem.at[1])
    routes_copy = pltpu.make_async_copy(routes_hbm, routes_ref, in_sem.at[2])
    routes_copy.start()
    s_copy.start()
    x_copy.start()
    for dy, dx in FACE:
        to_y, to_x = lax.rem(y + dy, 4), lax.rem(tile + dx, 4)
        face_peers.append((to_y * 4 + to_x, ((z * 4 + to_y) * 2 + core, to_x)))
        pl.semaphore_signal(barrier, inc=1, device_id=face_peers[-1][1], device_id_type=MESH)

    routes_copy.wait()
    masks = [jnp.int32(0)] * TILES
    for j in range(32):
        route = routes_ref[0, j]
        bit = (1 << j) if j < 31 else -(1 << 31)
        masks = [jnp.where(route == o, m | jnp.int32(bit), m) for o, m in enumerate(masks)]
    for o in range(TILES):
        m = masks[o]
        for k in range(SEND):
            low = m & (-m)
            table_ref[o, k] = jnp.where(m != 0, 31 - lax.clz(low), -1)
            m = m & (m - 1)

    s_copy.wait()
    x_copy.wait()
    cells = x_ref.shape[0] * 128
    sk = jnp.dot(x_ref[...].reshape(cells, 256), s_ref[...], preferred_element_type=F32).astype(BF16)
    sk_ref[...] = sk.reshape(sk_ref.shape)

    def all_of(ref, sem):
        return pltpu.make_async_copy(ref.at[pl.ds(0, GROUP - 1)], ref.at[pl.ds(0, GROUP - 1)], sem)

    def pick(o, k):
        at = table_ref[o, k]
        block = sk_ref[jnp.maximum(at, 0)]
        return jnp.where(at >= 0, block, jnp.zeros_like(block))

    parts = [part for step in START for part in step]

    def transfer(d, first, count):
        at = parts.index((d, first, count))
        return pltpu.make_async_remote_copy(
            src_ref=send_ref.at[d - 1, pl.ds(first, count)],
            dst_ref=placed_ref.at[tile, pl.ds(first, count)],
            send_sem=put_sem.at[at],
            recv_sem=get_sem.at[at],
            device_id=(slab, (tile + d) % TILES),
            device_id_type=MESH,
        )

    def fill(d, first, count):
        @pl.loop(first, first + count)
        def _(k):
            send_ref[d - 1, k] = pick((tile + d) % TILES, k)

    def begin(step):
        for part in START[step]:
            transfer(*part).start()

    gram = lax.dot_general(sk, sk, (((0,), (0,)), ((), ())), preferred_element_type=F32)
    part_ref[...] = gram.reshape(part_ref.shape)
    for part in START[0]:
        fill(*part)
    pl.semaphore_wait(barrier, 2 * (GROUP - 1))

    begin(0)
    for i, (to, peer) in enumerate(ring_peers):
        pltpu.make_async_remote_copy(
            src_ref=part_ref.at[to], dst_ref=got1_ref.at[i], send_sem=ar_put.at[0], recv_sem=ar_get.at[0],
            device_id=peer, device_id_type=MESH).start()

    for part in START[1] + START[2]:
        fill(*part)

    @pl.loop(0, SEND)
    def _(k):
        placed_ref[tile, k] = pick(tile, k)

    all_of(got1_ref, ar_get.at[0]).wait()
    got2_ref[face] = total_of([part_ref[ring]] + [got1_ref[i] for i in range(GROUP - 1)])
    for _, peer in face_peers:
        pltpu.make_async_remote_copy(
            src_ref=got2_ref.at[face], dst_ref=got2_ref.at[face], send_sem=ar_put.at[1], recv_sem=ar_get.at[1],
            device_id=peer, device_id_type=MESH).start()
    begin(1)
    all_of(got2_ref, ar_get.at[1]).wait()
    sum_ref[...] = total_of([got2_ref[i] for i in range(GROUP)])
    half = ring // (GROUP // 2)
    for _, peer in ring_peers:
        pltpu.make_async_remote_copy(
            src_ref=sum_ref, dst_ref=gram_ref.at[ring], send_sem=ar_put.at[2], recv_sem=half_get.at[half],
            device_id=peer, device_id_type=MESH).start()
    pltpu.make_async_copy(sum_ref, gram_ref.at[ring], half_get.at[half]).start()
    begin(2)

    def arrive(i):
        part = gram_ref.at[pl.ds(i * (GROUP // 2), GROUP // 2)]
        pltpu.make_async_copy(part, part, half_get.at[i]).wait()

    factor(gram_ref, upper_ref, inverse_ref, arrive)

    for i in range(3):
        all_of(got1_ref, ar_put.at[i]).wait()
    for part in parts:
        transfer(*part).wait()


def scale(cell_root, placed_ref, upper_ref, inverse_ref, basis_hbm, triangle_hbm, basis_ref, triangle_ref, sem, tri_sem):
    row = lax.broadcasted_iota(jnp.int32, (128, 128), 0)
    col = lax.broadcasted_iota(jnp.int32, (128, 128), 1)
    triangle_ref[...] = jnp.where(row <= col, upper_ref[...] * (1.0 / cell_root), 0.0)
    tri = pltpu.make_async_copy(triangle_ref, triangle_hbm, tri_sem)
    tri.start()
    h, m, _ = split3(jnp.where(row >= col, inverse_ref[...] * cell_root, 0.0))
    count = placed_ref.shape[0] // STEPS

    def copy(i):
        part = pl.ds(i * count, count)
        return pltpu.make_async_copy(basis_ref.at[part], basis_hbm.at[part], sem.at[i])

    for i in range(STEPS):
        part = pl.ds(i * count, count)
        rows = placed_ref[part].reshape(count * 128, 128)
        out = sum(lax.dot_general(rows, w, (((1,), (1,)), ((), ())), preferred_element_type=F32) for w in (m, h))
        basis_ref[part] = out.astype(BF16).reshape(count, 128, 128)
        copy(i).start()
    tri.wait()
    for i in range(STEPS):
        copy(i).wait()


def local(snapshots, routes, sketch_matrix):
    cell_root = math.sqrt(snapshots.shape[0] * 128 * lax.axis_size("slab") * lax.axis_size("tile"))
    vmem = pl.BlockSpec(memory_space=pltpu.VMEM)
    hbm = pl.BlockSpec(memory_space=pltpu.HBM)
    square = jax.ShapeDtypeStruct((128, 128), F32)
    placed, upper, inverse = pl.pallas_call(
        exchange,
        out_shape=(jax.ShapeDtypeStruct((TILES, SEND, 128, 128), BF16), square, square),
        in_specs=[hbm, hbm, hbm],
        out_specs=(vmem, vmem, vmem),
        scratch_shapes=[
            pltpu.VMEM((32, 128, 256), BF16),
            pltpu.VMEM((256, 128), BF16),
            pltpu.SMEM((1, 32), jnp.int32),
            pltpu.VMEM((32, 128, 128), BF16),
            pltpu.VMEM((TILES - 1, SEND, 128, 128), BF16),
            pltpu.VMEM((GROUP, 8, 128), F32),
            pltpu.VMEM((GROUP, 8, 128), F32),
            pltpu.VMEM((GROUP, 8, 128), F32),
            pltpu.VMEM((GROUP, 8, 128), F32),
            pltpu.VMEM((8, 128), F32),
            pltpu.SMEM((TILES, SEND), jnp.int32),
            pltpu.SemaphoreType.DMA((3,)),
            pltpu.SemaphoreType.DMA((sum(map(len, START)),)),
            pltpu.SemaphoreType.DMA((sum(map(len, START)),)),
            pltpu.SemaphoreType.DMA((3,)),
            pltpu.SemaphoreType.DMA((2,)),
            pltpu.SemaphoreType.DMA((2,)),
        ],
        compiler_params=pltpu.CompilerParams(collective_id=0, has_side_effects=True, vmem_limit_bytes=32 * 2**20),
        name="exchange",
    )(*(pltpu.with_memory_space_constraint(v, pltpu.HBM) for v in (routes.reshape(1, 32), snapshots, sketch_matrix)))
    return tuple(pl.pallas_call(
        lambda *refs: scale(cell_root, *refs),
        out_shape=(jax.ShapeDtypeStruct((TILES * SEND, 128, 128), BF16), square),
        in_specs=[vmem, vmem, vmem],
        out_specs=(hbm, hbm),
        scratch_shapes=[
            pltpu.VMEM((TILES * SEND, 128, 128), BF16),
            pltpu.VMEM((128, 128), F32),
            pltpu.SemaphoreType.DMA((STEPS,)),
            pltpu.SemaphoreType.DMA,
        ],
        compiler_params=pltpu.CompilerParams(vmem_limit_bytes=32 * 2**20),
        name="scale",
    )(placed.reshape(TILES * SEND, 128, 128), upper, inverse))


def solution(mesh):
    return jax.shard_map(
        local,
        mesh=mesh,
        in_specs=(P(("slab", "tile"), None, None), P(("slab", "tile"), None), P()),
        out_specs=(P(("slab", "tile"), None, None), P()),
        check_vma=False,
    )
```

```python
import math

import jax
import jax.numpy as jnp
from jax import lax
from jax.experimental import pallas as pl
from jax.experimental.pallas import tpu as pltpu
from jax.sharding import PartitionSpec as P

SEND = 10
TILES = 4
GROUP = 16
STEPS = 8
SPAN = 32
PANELS = SPAN // 8
START = (((2, 0, 7),), ((1, 0, 10), (3, 0, 10)), ((2, 7, 3),))
RING = sorted(((dz, dc) for dz in range(8) for dc in range(2) if dz or dc), key=lambda d: -2 * min(d[0], 8 - d[0]) - d[1])
FACE = sorted(((dy, dx) for dy in range(4) for dx in range(4) if dy or dx), key=lambda d: -sum(min(v, 4 - v) for v in d))
MESH = pl.DeviceIdType.MESH
F32, BF16 = jnp.float32, jnp.bfloat16


def split3(v):
    h = v.astype(BF16)
    rest = v - h.astype(F32)
    m = rest.astype(BF16)
    return h, m, (rest - m.astype(F32)).astype(BF16)


def outer_products(u):
    h, m, l = split3(u)
    left = jnp.concatenate([v[:, :128] for v in (h, h, m, h, l, m)], 0)
    right = jnp.concatenate([h, m, h, l, h, m], 0)
    return lax.dot_general(left, right, (((0,), (0,)), ((), ())), preferred_element_type=F32)


def line(v, i):
    return jnp.broadcast_to(v[i : i + 1], (8, v.shape[1]))


def columns(rows, p):
    return [jnp.broadcast_to(rows[:, p + k : p + k + 1], (8, 128)) for k in range(8)]


def wide(v):
    return jnp.concatenate([v, v], 1)


def factor(gram_ref, upper_ref, inverse_ref, arrive):
    row = lax.broadcasted_iota(jnp.int32, (8, 128), 0)
    col = lax.broadcasted_iota(jnp.int32, (8, 128), 1)
    sub = lax.broadcasted_iota(jnp.int32, (8, 256), 0)
    product = None
    for s in range(0, 128, SPAN):
        arrive(s // SPAN)
        rows = {q: jnp.concatenate([gram_ref[q // 8], (row + q == col).astype(F32)], 1) for q in range(s, s + SPAN, 8)}
        if s:
            rows = {q: v - product[q : q + 8] for q, v in rows.items()}
        own = columns(rows[s], s)
        done = []
        for p in range(s, s + SPAN, 8):
            later = range(p + 8, s + SPAN, 8)
            cols = {q: columns(rows[q], p) for q in later}
            e = {(i, k): line(own[k], i) for k in range(8) for i in range(k, 8)}
            own = columns(rows[p + 8], p + 8) if later else None
            x = [line(rows[p], i) for i in range(8)]
            for k in range(8):
                r = lax.rsqrt(e[k, k])
                l = {i: e[i, k] * r for i in range(k + 1, 8)}
                for i in range(k + 1, 8):
                    for j in range(k + 1, i + 1):
                        e[i, j] = e[i, j] - l[i] * l[j]
                x[k] = x[k] * wide(r)
                for i in range(k + 1, 8):
                    x[i] = x[i] - wide(l[i]) * x[k]
                for q in later:
                    m = cols[q][k] * r
                    if q == p + 8:
                        own = [o - m * line(m, j) for j, o in enumerate(own)]
                    for j in range(k + 1, 8):
                        cols[q][j] = cols[q][j] - m * l[j]
                    rows[q] = rows[q] - wide(m) * x[k]
            u = x[0]
            for k in range(1, 8):
                u = jnp.where(sub == k, x[k], u)
            upper_ref[p : p + 8, :] = u[:, :128]
            inverse_ref[p : p + 8, :] = u[:, 128:]
            done.append(u)
        if s + SPAN < 128:
            new = outer_products(jnp.concatenate(done, 0))
            product = new if product is None else product + new


def total_of(terms):
    while len(terms) > 1:
        terms = [sum(terms[i : i + 2]) for i in range(0, len(terms), 2)]
    return terms[0]


def exchange(routes_hbm, x_hbm, s_hbm, placed_ref, upper_ref, inverse_ref, x_ref, s_ref, routes_ref, sk_ref, send_ref, part_ref,
             got1_ref, got2_ref, gram_ref, sum_ref, table_ref, in_sem, put_sem, get_sem, ar_put, ar_get, share_get):
    slab, tile = lax.axis_index("slab"), lax.axis_index("tile")
    core, y, z = slab % 2, (slab // 2) % 4, slab // 8
    ring = z * 2 + core
    face = y * 4 + tile

    barrier = pltpu.get_barrier_semaphore()
    ring_peers, face_peers = [], []
    for dz, dc in RING:
        to_z, to_core = lax.rem(z + dz, 8), lax.rem(core + dc, 2)
        ring_peers.append((to_z * 2 + to_core, ((to_z * 4 + y) * 2 + to_core, tile)))
        pl.semaphore_signal(barrier, inc=1, device_id=ring_peers[-1][1], device_id_type=MESH)
    x_copy = pltpu.make_async_copy(x_hbm, x_ref, in_sem.at[0])
    s_copy = pltpu.make_async_copy(s_hbm, s_ref, in_sem.at[1])
    routes_copy = pltpu.make_async_copy(routes_hbm, routes_ref, in_sem.at[2])
    routes_copy.start()
    s_copy.start()
    x_copy.start()
    for dy, dx in FACE:
        to_y, to_x = lax.rem(y + dy, 4), lax.rem(tile + dx, 4)
        face_peers.append((to_y * 4 + to_x, ((z * 4 + to_y) * 2 + core, to_x)))
        pl.semaphore_signal(barrier, inc=1, device_id=face_peers[-1][1], device_id_type=MESH)

    routes_copy.wait()
    masks = [jnp.int32(0)] * TILES
    for j in range(32):
        route = routes_ref[0, j]
        bit = (1 << j) if j < 31 else -(1 << 31)
        masks = [jnp.where(route == o, m | jnp.int32(bit), m) for o, m in enumerate(masks)]
    for o in range(TILES):
        m = masks[o]
        for k in range(SEND):
            low = m & (-m)
            table_ref[o, k] = jnp.where(m != 0, 31 - lax.clz(low), -1)
            m = m & (m - 1)

    s_copy.wait()
    x_copy.wait()
    cells = x_ref.shape[0] * 128
    sk = jnp.dot(x_ref[...].reshape(cells, 256), s_ref[...], preferred_element_type=F32).astype(BF16)
    sk_ref[...] = sk.reshape(sk_ref.shape)

    def all_of(ref, sem):
        return pltpu.make_async_copy(ref.at[pl.ds(0, GROUP - 1)], ref.at[pl.ds(0, GROUP - 1)], sem)

    def pick(o, k):
        at = table_ref[o, k]
        block = sk_ref[jnp.maximum(at, 0)]
        return jnp.where(at >= 0, block, jnp.zeros_like(block))

    parts = [part for step in START for part in step]

    def transfer(d, first, count):
        at = parts.index((d, first, count))
        return pltpu.make_async_remote_copy(
            src_ref=send_ref.at[d - 1, pl.ds(first, count)],
            dst_ref=placed_ref.at[tile, pl.ds(first, count)],
            send_sem=put_sem.at[at],
            recv_sem=get_sem.at[at],
            device_id=(slab, (tile + d) % TILES),
            device_id_type=MESH,
        )

    def fill(d, first, count):
        @pl.loop(first, first + count)
        def _(k):
            send_ref[d - 1, k] = pick((tile + d) % TILES, k)

    def begin(step):
        for part in START[step]:
            transfer(*part).start()

    gram = lax.dot_general(sk, sk, (((0,), (0,)), ((), ())), preferred_element_type=F32)
    part_ref[...] = gram.reshape(part_ref.shape)
    for part in START[0]:
        fill(*part)
    pl.semaphore_wait(barrier, 2 * (GROUP - 1))

    begin(0)
    for i, (to, peer) in enumerate(ring_peers):
        pltpu.make_async_remote_copy(
            src_ref=part_ref.at[to], dst_ref=got1_ref.at[i], send_sem=ar_put.at[0], recv_sem=ar_get.at[0],
            device_id=peer, device_id_type=MESH).start()

    for part in START[1] + START[2]:
        fill(*part)

    @pl.loop(0, SEND)
    def _(k):
        placed_ref[tile, k] = pick(tile, k)

    all_of(got1_ref, ar_get.at[0]).wait()
    got2_ref[face] = total_of([part_ref[ring]] + [got1_ref[i] for i in range(GROUP - 1)])
    for _, peer in face_peers:
        pltpu.make_async_remote_copy(
            src_ref=got2_ref.at[face], dst_ref=got2_ref.at[face], send_sem=ar_put.at[1], recv_sem=ar_get.at[1],
            device_id=peer, device_id_type=MESH).start()
    begin(1)
    all_of(got2_ref, ar_get.at[1]).wait()
    sum_ref[...] = total_of([got2_ref[i] for i in range(GROUP)])
    share = ring // PANELS
    for _, peer in ring_peers:
        pltpu.make_async_remote_copy(
            src_ref=sum_ref, dst_ref=gram_ref.at[ring], send_sem=ar_put.at[2], recv_sem=share_get.at[share],
            device_id=peer, device_id_type=MESH).start()
    pltpu.make_async_copy(sum_ref, gram_ref.at[ring], share_get.at[share]).start()
    begin(2)

    def arrive(i):
        part = gram_ref.at[pl.ds(i * PANELS, PANELS)]
        pltpu.make_async_copy(part, part, share_get.at[i]).wait()

    factor(gram_ref, upper_ref, inverse_ref, arrive)

    for i in range(3):
        all_of(got1_ref, ar_put.at[i]).wait()
    for part in parts:
        transfer(*part).wait()


def scale(cell_root, placed_ref, upper_ref, inverse_ref, basis_hbm, triangle_hbm, basis_ref, triangle_ref, sem, tri_sem):
    row = lax.broadcasted_iota(jnp.int32, (128, 128), 0)
    col = lax.broadcasted_iota(jnp.int32, (128, 128), 1)
    triangle_ref[...] = jnp.where(row <= col, upper_ref[...] * (1.0 / cell_root), 0.0)
    tri = pltpu.make_async_copy(triangle_ref, triangle_hbm, tri_sem)
    tri.start()
    h, m, _ = split3(jnp.where(row >= col, inverse_ref[...] * cell_root, 0.0))
    count = placed_ref.shape[0] // STEPS

    def copy(i):
        part = pl.ds(i * count, count)
        return pltpu.make_async_copy(basis_ref.at[part], basis_hbm.at[part], sem.at[i])

    for i in range(STEPS):
        part = pl.ds(i * count, count)
        rows = placed_ref[part].reshape(count * 128, 128)
        out = sum(lax.dot_general(rows, w, (((1,), (1,)), ((), ())), preferred_element_type=F32) for w in (m, h))
        basis_ref[part] = out.astype(BF16).reshape(count, 128, 128)
        copy(i).start()
    tri.wait()
    for i in range(STEPS):
        copy(i).wait()


def local(snapshots, routes, sketch_matrix):
    cell_root = math.sqrt(snapshots.shape[0] * 128 * lax.axis_size("slab") * lax.axis_size("tile"))
    vmem = pl.BlockSpec(memory_space=pltpu.VMEM)
    hbm = pl.BlockSpec(memory_space=pltpu.HBM)
    square = jax.ShapeDtypeStruct((128, 128), F32)
    placed, upper, inverse = pl.pallas_call(
        exchange,
        out_shape=(jax.ShapeDtypeStruct((TILES, SEND, 128, 128), BF16), square, square),
        in_specs=[hbm, hbm, hbm],
        out_specs=(vmem, vmem, vmem),
        scratch_shapes=[
            pltpu.VMEM((32, 128, 256), BF16),
            pltpu.VMEM((256, 128), BF16),
            pltpu.SMEM((1, 32), jnp.int32),
            pltpu.VMEM((32, 128, 128), BF16),
            pltpu.VMEM((TILES - 1, SEND, 128, 128), BF16),
            pltpu.VMEM((GROUP, 8, 128), F32),
            pltpu.VMEM((GROUP, 8, 128), F32),
            pltpu.VMEM((GROUP, 8, 128), F32),
            pltpu.VMEM((GROUP, 8, 128), F32),
            pltpu.VMEM((8, 128), F32),
            pltpu.SMEM((TILES, SEND), jnp.int32),
            pltpu.SemaphoreType.DMA((3,)),
            pltpu.SemaphoreType.DMA((sum(map(len, START)),)),
            pltpu.SemaphoreType.DMA((sum(map(len, START)),)),
            pltpu.SemaphoreType.DMA((3,)),
            pltpu.SemaphoreType.DMA((2,)),
            pltpu.SemaphoreType.DMA((GROUP // PANELS,)),
        ],
        compiler_params=pltpu.CompilerParams(collective_id=0, has_side_effects=True, vmem_limit_bytes=32 * 2**20),
        name="exchange",
    )(*(pltpu.with_memory_space_constraint(v, pltpu.HBM) for v in (routes.reshape(1, 32), snapshots, sketch_matrix)))
    return tuple(pl.pallas_call(
        lambda *refs: scale(cell_root, *refs),
        out_shape=(jax.ShapeDtypeStruct((TILES * SEND, 128, 128), BF16), square),
        in_specs=[vmem, vmem, vmem],
        out_specs=(hbm, hbm),
        scratch_shapes=[
            pltpu.VMEM((TILES * SEND, 128, 128), BF16),
            pltpu.VMEM((128, 128), F32),
            pltpu.SemaphoreType.DMA((STEPS,)),
            pltpu.SemaphoreType.DMA,
        ],
        compiler_params=pltpu.CompilerParams(vmem_limit_bytes=32 * 2**20),
        name="scale",
    )(placed.reshape(TILES * SEND, 128, 128), upper, inverse))


def solution(mesh):
    return jax.shard_map(
        local,
        mesh=mesh,
        in_specs=(P(("slab", "tile"), None, None), P(("slab", "tile"), None), P()),
        out_specs=(P(("slab", "tile"), None, None), P()),
        check_vma=False,
    )
```

```python
import math

import jax
import jax.numpy as jnp
from jax import lax
from jax.experimental import pallas as pl
from jax.experimental.pallas import tpu as pltpu
from jax.sharding import PartitionSpec as P

SEND = 10
TILES = 4
GROUP = 16
STEPS = 8
SPAN = 32
PANELS = SPAN // 8
START = (((2, 0, 7),), ((1, 0, 10), (3, 0, 10)), ((2, 7, 3),))
RING = sorted(((dz, dc) for dz in range(8) for dc in range(2) if dz or dc), key=lambda d: -2 * min(d[0], 8 - d[0]) - d[1])
FACE = sorted(((dy, dx) for dy in range(4) for dx in range(4) if dy or dx), key=lambda d: -sum(min(v, 4 - v) for v in d))
MESH = pl.DeviceIdType.MESH
F32, BF16 = jnp.float32, jnp.bfloat16


def split3(v):
    h = v.astype(BF16)
    rest = v - h.astype(F32)
    m = rest.astype(BF16)
    return h, m, (rest - m.astype(F32)).astype(BF16)


def outer_products(u):
    h, m, l = split3(u)
    left = jnp.concatenate([v[:, :128] for v in (h, h, m, h, l, m)], 0)
    right = jnp.concatenate([h, m, h, l, h, m], 0)
    return lax.dot_general(left, right, (((0,), (0,)), ((), ())), preferred_element_type=F32)


def line(v, i):
    return jnp.broadcast_to(v[i : i + 1], (8, v.shape[1]))


def columns(rows, p):
    return [jnp.broadcast_to(rows[:, p + k : p + k + 1], (8, 128)) for k in range(8)]


def wide(v):
    return jnp.concatenate([v, v], 1)


def factor(gram_ref, upper_ref, inverse_ref, arrive):
    row = lax.broadcasted_iota(jnp.int32, (8, 128), 0)
    col = lax.broadcasted_iota(jnp.int32, (8, 128), 1)
    sub = lax.broadcasted_iota(jnp.int32, (8, 256), 0)
    product = None
    for s in range(0, 128, SPAN):
        arrive(s // SPAN)
        rows = {q: jnp.concatenate([gram_ref[q // 8], (row + q == col).astype(F32)], 1) for q in range(s, s + SPAN, 8)}
        if s:
            rows = {q: v - product[q : q + 8] for q, v in rows.items()}
        own = columns(rows[s], s)
        done = []
        for p in range(s, s + SPAN, 8):
            later = range(p + 8, s + SPAN, 8)
            cols = {q: columns(rows[q], p) for q in later}
            e = {(i, k): line(own[k], i) for k in range(8) for i in range(k, 8)}
            own = columns(rows[p + 8], p + 8) if later else None
            x = [line(rows[p], i) for i in range(8)]
            for k in range(8):
                r = lax.rsqrt(e[k, k])
                l = {i: e[i, k] * r for i in range(k + 1, 8)}
                for i in range(k + 1, 8):
                    for j in range(k + 1, i + 1):
                        e[i, j] = e[i, j] - l[i] * l[j]
                x[k] = x[k] * wide(r)
                for i in range(k + 1, 8):
                    x[i] = x[i] - wide(l[i]) * x[k]
                for q in later:
                    m = cols[q][k] * r
                    if q == p + 8:
                        own = [o - m * line(m, j) for j, o in enumerate(own)]
                    for j in range(k + 1, 8):
                        cols[q][j] = cols[q][j] - m * l[j]
                    rows[q] = rows[q] - wide(m) * x[k]
            u = x[0]
            for k in range(1, 8):
                u = jnp.where(sub == k, x[k], u)
            upper_ref[p : p + 8, :] = u[:, :128]
            inverse_ref[p : p + 8, :] = u[:, 128:]
            done.append(u)
        if s + SPAN < 128:
            new = outer_products(jnp.concatenate(done, 0))
            product = new if product is None else product + new


def total_of(terms):
    while len(terms) > 1:
        terms = [sum(terms[i : i + 2]) for i in range(0, len(terms), 2)]
    return terms[0]


def exchange(routes_hbm, x_hbm, s_hbm, placed_ref, upper_ref, inverse_ref, x_ref, s_ref, routes_ref, sk_ref, send_ref, part_ref,
             got1_ref, got2_ref, gram_ref, sum_ref, table_ref, in_sem, put_sem, get_sem, ar_put, ar_get, share_get):
    slab, tile = lax.axis_index("slab"), lax.axis_index("tile")
    core, y, z = slab % 2, (slab // 2) % 4, slab // 8
    ring = z * 2 + core
    face = y * 4 + tile

    barrier = pltpu.get_barrier_semaphore()
    ring_peers, face_peers = [], []
    for dz, dc in RING:
        to_z, to_core = lax.rem(z + dz, 8), lax.rem(core + dc, 2)
        ring_peers.append((to_z * 2 + to_core, ((to_z * 4 + y) * 2 + to_core, tile)))
        pl.semaphore_signal(barrier, inc=1, device_id=ring_peers[-1][1], device_id_type=MESH)
    x_copy = pltpu.make_async_copy(x_hbm, x_ref, in_sem.at[0])
    s_copy = pltpu.make_async_copy(s_hbm, s_ref, in_sem.at[1])
    routes_copy = pltpu.make_async_copy(routes_hbm, routes_ref, in_sem.at[2])
    routes_copy.start()
    s_copy.start()
    x_copy.start()
    for dy, dx in FACE:
        to_y, to_x = lax.rem(y + dy, 4), lax.rem(tile + dx, 4)
        face_peers.append((to_y * 4 + to_x, ((z * 4 + to_y) * 2 + core, to_x)))
        pl.semaphore_signal(barrier, inc=1, device_id=face_peers[-1][1], device_id_type=MESH)

    routes_copy.wait()
    masks = [jnp.int32(0)] * TILES
    for j in range(32):
        route = routes_ref[0, j]
        bit = (1 << j) if j < 31 else -(1 << 31)
        masks = [jnp.where(route == o, m | jnp.int32(bit), m) for o, m in enumerate(masks)]
    for o in range(TILES):
        m = masks[o]
        for k in range(SEND):
            low = m & (-m)
            table_ref[o, k] = jnp.where(m != 0, 31 - lax.clz(low), -1)
            m = m & (m - 1)

    s_copy.wait()
    x_copy.wait()
    cells = x_ref.shape[0] * 128
    sk = jnp.dot(x_ref[...].reshape(cells, 256), s_ref[...], preferred_element_type=F32).astype(BF16)
    sk_ref[...] = sk.reshape(sk_ref.shape)

    def all_of(ref, sem):
        return pltpu.make_async_copy(ref.at[pl.ds(0, GROUP - 1)], ref.at[pl.ds(0, GROUP - 1)], sem)

    def pick(o, k):
        at = table_ref[o, k]
        block = sk_ref[jnp.maximum(at, 0)]
        return jnp.where(at >= 0, block, jnp.zeros_like(block))

    parts = [part for step in START for part in step]

    def transfer(d, first, count):
        at = parts.index((d, first, count))
        return pltpu.make_async_remote_copy(
            src_ref=send_ref.at[d - 1, pl.ds(first, count)],
            dst_ref=placed_ref.at[tile, pl.ds(first, count)],
            send_sem=put_sem.at[at],
            recv_sem=get_sem.at[at],
            device_id=(slab, (tile + d) % TILES),
            device_id_type=MESH,
        )

    def fill(d, first, count, unroll=1):
        @pl.loop(first, first + count, unroll=unroll)
        def _(k):
            send_ref[d - 1, k] = pick((tile + d) % TILES, k)

    def begin(step):
        for part in START[step]:
            transfer(*part).start()

    gram = lax.dot_general(sk, sk, (((0,), (0,)), ((), ())), preferred_element_type=F32)
    part_ref[...] = gram.reshape(part_ref.shape)
    for part in START[0]:
        fill(*part, unroll=part[2])
    pl.semaphore_wait(barrier, 2 * (GROUP - 1))

    begin(0)
    for i, (to, peer) in enumerate(ring_peers):
        pltpu.make_async_remote_copy(
            src_ref=part_ref.at[to], dst_ref=got1_ref.at[i], send_sem=ar_put.at[0], recv_sem=ar_get.at[0],
            device_id=peer, device_id_type=MESH).start()

    for part in START[1] + START[2]:
        fill(*part)

    @pl.loop(0, SEND)
    def _(k):
        placed_ref[tile, k] = pick(tile, k)

    all_of(got1_ref, ar_get.at[0]).wait()
    got2_ref[face] = total_of([part_ref[ring]] + [got1_ref[i] for i in range(GROUP - 1)])
    for _, peer in face_peers:
        pltpu.make_async_remote_copy(
            src_ref=got2_ref.at[face], dst_ref=got2_ref.at[face], send_sem=ar_put.at[1], recv_sem=ar_get.at[1],
            device_id=peer, device_id_type=MESH).start()
    begin(1)
    all_of(got2_ref, ar_get.at[1]).wait()
    sum_ref[...] = total_of([got2_ref[i] for i in range(GROUP)])
    share = ring // PANELS
    for _, peer in ring_peers:
        pltpu.make_async_remote_copy(
            src_ref=sum_ref, dst_ref=gram_ref.at[ring], send_sem=ar_put.at[2], recv_sem=share_get.at[share],
            device_id=peer, device_id_type=MESH).start()
    pltpu.make_async_copy(sum_ref, gram_ref.at[ring], share_get.at[share]).start()
    begin(2)

    def arrive(i):
        part = gram_ref.at[pl.ds(i * PANELS, PANELS)]
        pltpu.make_async_copy(part, part, share_get.at[i]).wait()

    factor(gram_ref, upper_ref, inverse_ref, arrive)

    for i in range(3):
        all_of(got1_ref, ar_put.at[i]).wait()
    for part in parts:
        transfer(*part).wait()


def scale(cell_root, placed_ref, upper_ref, inverse_ref, basis_hbm, triangle_hbm, basis_ref, triangle_ref, sem, tri_sem):
    row = lax.broadcasted_iota(jnp.int32, (128, 128), 0)
    col = lax.broadcasted_iota(jnp.int32, (128, 128), 1)
    triangle_ref[...] = jnp.where(row <= col, upper_ref[...] * (1.0 / cell_root), 0.0)
    tri = pltpu.make_async_copy(triangle_ref, triangle_hbm, tri_sem)
    tri.start()
    h, m, _ = split3(jnp.where(row >= col, inverse_ref[...] * cell_root, 0.0))
    count = placed_ref.shape[0] // STEPS

    def copy(i):
        part = pl.ds(i * count, count)
        return pltpu.make_async_copy(basis_ref.at[part], basis_hbm.at[part], sem.at[i])

    for i in range(STEPS):
        part = pl.ds(i * count, count)
        rows = placed_ref[part].reshape(count * 128, 128)
        out = sum(lax.dot_general(rows, w, (((1,), (1,)), ((), ())), preferred_element_type=F32) for w in (m, h))
        basis_ref[part] = out.astype(BF16).reshape(count, 128, 128)
        copy(i).start()
    tri.wait()
    for i in range(STEPS):
        copy(i).wait()


def local(snapshots, routes, sketch_matrix):
    cell_root = math.sqrt(snapshots.shape[0] * 128 * lax.axis_size("slab") * lax.axis_size("tile"))
    vmem = pl.BlockSpec(memory_space=pltpu.VMEM)
    hbm = pl.BlockSpec(memory_space=pltpu.HBM)
    square = jax.ShapeDtypeStruct((128, 128), F32)
    placed, upper, inverse = pl.pallas_call(
        exchange,
        out_shape=(jax.ShapeDtypeStruct((TILES, SEND, 128, 128), BF16), square, square),
        in_specs=[hbm, hbm, hbm],
        out_specs=(vmem, vmem, vmem),
        scratch_shapes=[
            pltpu.VMEM((32, 128, 256), BF16),
            pltpu.VMEM((256, 128), BF16),
            pltpu.SMEM((1, 32), jnp.int32),
            pltpu.VMEM((32, 128, 128), BF16),
            pltpu.VMEM((TILES - 1, SEND, 128, 128), BF16),
            pltpu.VMEM((GROUP, 8, 128), F32),
            pltpu.VMEM((GROUP, 8, 128), F32),
            pltpu.VMEM((GROUP, 8, 128), F32),
            pltpu.VMEM((GROUP, 8, 128), F32),
            pltpu.VMEM((8, 128), F32),
            pltpu.SMEM((TILES, SEND), jnp.int32),
            pltpu.SemaphoreType.DMA((3,)),
            pltpu.SemaphoreType.DMA((sum(map(len, START)),)),
            pltpu.SemaphoreType.DMA((sum(map(len, START)),)),
            pltpu.SemaphoreType.DMA((3,)),
            pltpu.SemaphoreType.DMA((2,)),
            pltpu.SemaphoreType.DMA((GROUP // PANELS,)),
        ],
        compiler_params=pltpu.CompilerParams(collective_id=0, has_side_effects=True, vmem_limit_bytes=32 * 2**20),
        name="exchange",
    )(*(pltpu.with_memory_space_constraint(v, pltpu.HBM) for v in (routes.reshape(1, 32), snapshots, sketch_matrix)))
    return tuple(pl.pallas_call(
        lambda *refs: scale(cell_root, *refs),
        out_shape=(jax.ShapeDtypeStruct((TILES * SEND, 128, 128), BF16), square),
        in_specs=[vmem, vmem, vmem],
        out_specs=(hbm, hbm),
        scratch_shapes=[
            pltpu.VMEM((TILES * SEND, 128, 128), BF16),
            pltpu.VMEM((128, 128), F32),
            pltpu.SemaphoreType.DMA((STEPS,)),
            pltpu.SemaphoreType.DMA,
        ],
        compiler_params=pltpu.CompilerParams(vmem_limit_bytes=32 * 2**20),
        name="scale",
    )(placed.reshape(TILES * SEND, 128, 128), upper, inverse))


def solution(mesh):
    return jax.shard_map(
        local,
        mesh=mesh,
        in_specs=(P(("slab", "tile"), None, None), P(("slab", "tile"), None), P()),
        out_specs=(P(("slab", "tile"), None, None), P()),
        check_vma=False,
    )
```
